32 devices in a mesh: outer: 2 (over x), inner: 4 (over z), tensor: 4 (over y, core).
Axes of the slice: x: 2, y: 2, z: 4, core: 2. Of those that a mesh axis runs over, the one named last changes fastest.
Arguments:
- queries: bfloat16 [2048, 16, 128], P(('outer', 'inner'), 'tensor'), may hold values from -5 to 5
- keys: bfloat16 [2048, 4, 128], P(('outer', 'inner'), 'tensor'), may hold values from -5 to 5
- values: bfloat16 [2048, 4, 128], P(('outer', 'inner'), 'tensor'), may hold values from -6 to 6
- w_out: bfloat16 [16, 128, 4096], P('tensor'), may hold values from -0.125 to 0.125
- d_out: bfloat16 [2048, 4096], P(('outer', 'inner', 'tensor')), may hold values from -6 to 6
- lengths: int32 [16], replicated, may hold values from 1 to 1280, 2048 in all
Outputs:
- mixed: bfloat16 [2048, 4096], P(('outer', 'inner', 'tensor'))
- d_queries: bfloat16 [2048, 16, 128], P(('outer', 'inner'), 'tensor')
- d_keys: bfloat16 [2048, 4, 128], P(('outer', 'inner'), 'tensor')
- d_values: bfloat16 [2048, 4, 128], P(('outer', 'inner'), 'tensor')
The draws below stay inside these ranges and needn't reach their ends.
Inputs may be any that keep to these rules, and one draw needn't show every extreme that they name: `lengths`: the 16 documents fill the sequence of 2048 tokens exactly, and the longest has exactly 1280 tokens.
All inputs are finite; a program needn't handle non-finite values.
Results may differ from the reference program's by a relative error of at most 0.04.
Values may be sent and summed in bfloat16 or wider, within the bound.
No kernel may reach another device: no remote copies, remote signals or barrier semaphores. Data moves between devices by JAX's collectives and lax.ppermute only.
A program may use at most 128 MiB of HBM per device.

```python
import math
import jax
import jax.numpy as jnp
import numpy as np
from jax import lax

D = 4096
HD = 128
HEADS = 16
KV_HEADS = 4
DOCS = 16
TOKENS = 2048
MOST_DOC = 1280


def drawn_pair(key):
    base_q = jnp.clip(jax.random.normal(jax.random.fold_in(key, 11), (TOKENS, HEADS, HD), jnp.float32), -5.0, 5.0)
    base_k = jnp.clip(jax.random.normal(jax.random.fold_in(key, 12), (TOKENS, KV_HEADS, HD), jnp.float32), -5.0, 5.0)
    return (base_q, base_k)


def draw_queries(key, part):
    return drawn_pair(key)[0].astype(jnp.bfloat16)


def draw_keys(key, part):
    return drawn_pair(key)[1].astype(jnp.bfloat16)


def levels(rng, shape, cuts, smallest, largest):
    def one(dim, shards_of):
        draws = jax.random.uniform(jax.random.fold_in(jax.random.fold_in(rng, 6), dim), (shards_of,), jnp.float32, smallest / len(cuts), largest / len(cuts))
        return jnp.repeat(jnp.exp(draws), shape[dim] // shards_of).reshape((-1,) + (1,) * (len(shape) - dim - 1))

    level = one(*cuts[0])
    for cut in cuts[1:]:
        level = level * one(*cut)
    return level


def length_profile(number_of, total, limit, lean):
    loads = [(1 << 20) // math.isqrt(standing ** lean) + 1 for standing in range(2, number_of + 1)]
    surplus, given = total - limit - (number_of - 1), [1] * (number_of - 1)
    while surplus > 0:
        free = [i for i in range(number_of - 1) if given[i] < limit]
        pool, remaining = sum([loads[i] for i in free]), surplus
        for i in free:
            more = min(limit - given[i], max(1, remaining * loads[i] // pool), surplus)
            given[i] = given[i] + more
            surplus = surplus - more
    return np.array([limit] + given)


def ragged_sizes(stream_key, number_of, total, most, slope):
    if number_of == 2:
        one = jax.random.randint(stream_key, (), max(1, total - most), min(most, total - 1) + 1)
        return jnp.stack([one, total - one])
    sizes = jnp.asarray(length_profile(number_of, total, most, slope), jnp.int32)
    couples = (number_of - 1) // 2
    source_of, taker = sizes[1:1 + 2 * couples:2], sizes[2:2 + 2 * couples:2]
    slack = jnp.minimum(source_of - 1, most - taker)
    shifted = jax.random.randint(jax.random.fold_in(stream_key, 1), (couples,), 0, 1 << 20) % (slack + 1)
    sizes = sizes.at[1:1 + 2 * couples:2].set(source_of - shifted).at[2:2 + 2 * couples:2].set(taker + shifted)
    return sizes[jax.random.permutation(jax.random.fold_in(stream_key, 2), number_of)]


def scatter_about(rng, dims, scale, reach, pieces=(), held_as=jnp.bfloat16):
    values = scale * jax.random.normal(rng, dims, jnp.float32)
    if pieces:
        values = values * levels(rng, dims, pieces, -0.22, 0.18)
    return jnp.clip(values, -reach, reach).astype(held_as)


def setup_inputs(seed: int = 0) -> dict:
    key_list = jax.random.split(jax.random.key(seed), 7)
    queries = draw_queries(jax.random.fold_in(key_list[6], 71), 0)
    keys = draw_keys(jax.random.fold_in(key_list[6], 71), 0)
    values = scatter_about(key_list[2], (TOKENS, KV_HEADS, HD), 1.0, 6.0, ((0, 8), (1, 4)))
    w_out = scatter_about(key_list[3], (HEADS, HD, D), (HEADS * HD) ** -0.5, 0.125, ((0, 4),))
    d_out = scatter_about(key_list[4], (TOKENS, D), 1.0, 6.0, ((0, 32),))
    lengths = ragged_sizes(key_list[5], DOCS, TOKENS, MOST_DOC, 2).astype(jnp.int32)
    return dict(queries=queries, keys=keys, values=values, w_out=w_out, d_out=d_out, lengths=lengths)


NEG_FILL = -1e30


def segment_of(positions, ends):
    return jnp.sum((positions[:, None] >= ends[None, :]).astype(jnp.int32), axis=1)


def doc_begin(position, ends):
    return jnp.max(jnp.where(ends <= position, ends, jnp.zeros_like(ends)))


def masked_scores(q_rows, k_block, q_pos, q_seg, k_start, ends, scale):
    width = k_block.shape[0]
    k_pos = k_start + jnp.arange(width, dtype=jnp.int32)
    k_seg = segment_of(k_pos, ends)
    s = lax.dot_general(q_rows, k_block, (((1,), (1,)), ((), ())), preferred_element_type=jnp.float32) * scale
    mask = (k_pos[None, :] <= q_pos[:, None]) & (k_seg[None, :] == q_seg[:, None])
    return jnp.where(mask, s, NEG_FILL), mask


def reference(queries, keys, values, w_out, d_out, lengths):
    group = HEADS // KV_HEADS
    scale = HD ** -0.5
    ends = jnp.cumsum(lengths).astype(jnp.int32)
    w_flat = w_out.reshape(HEADS * HD, D)
    d_attn = lax.dot_general(d_out, w_flat, (((1,), (1,)), ((), ())), preferred_element_type=jnp.float32).astype(jnp.bfloat16)
    span = math.gcd(512, TOKENS)
    n_blocks = TOKENS // span
    rows = span * group
    q_heads = queries.reshape(TOKENS, KV_HEADS, group, HD).transpose(1, 0, 2, 3).reshape(KV_HEADS, TOKENS * group, HD)
    g_heads = d_attn.reshape(TOKENS, KV_HEADS, group, HD).transpose(1, 0, 2, 3).reshape(KV_HEADS, TOKENS * group, HD)
    k_heads = keys.transpose(1, 0, 2)
    v_heads = values.transpose(1, 0, 2)

    def one_head(operands):
        q_all, g_all, k_all, v_all = operands

        def query_block(carry, index):
            dk_acc, dv_acc = carry
            q_start = (index * span).astype(jnp.int32)
            q_rows = lax.dynamic_slice_in_dim(q_all, q_start * group, rows, 0)
            g_rows = lax.dynamic_slice_in_dim(g_all, q_start * group, rows, 0)
            q_pos = q_start + jnp.arange(rows, dtype=jnp.int32) // group
            q_seg = segment_of(q_pos, ends)
            first = doc_begin(q_start, ends)
            last = q_start + span - 1

            def needed(b):
                k_start = b * span
                return (k_start <= last) & (k_start + span - 1 >= first)

            def scores_at(b):
                k_start = (b * span).astype(jnp.int32)
                k_block = lax.dynamic_slice_in_dim(k_all, k_start, span, 0)
                return masked_scores(q_rows, k_block, q_pos, q_seg, k_start, ends, scale)

            def stats(b, state):
                def work(st):
                    top, denom = st
                    s, mask = scores_at(b)
                    new_top = jnp.maximum(top, jnp.max(s, axis=1))
                    weights = jnp.where(mask, jnp.exp(s - new_top[:, None]), jnp.float32(0.0))
                    return new_top, denom * jnp.exp(top - new_top) + jnp.sum(weights, axis=1)
                return lax.cond(needed(b), work, lambda st: st, state)

            top, denom = lax.fori_loop(0, n_blocks, stats, (jnp.full((rows,), NEG_FILL, jnp.float32), jnp.zeros((rows,), jnp.float32)))
            lse = top + jnp.log(denom)

            def probs_at(b):
                s, mask = scores_at(b)
                return jnp.where(mask, jnp.exp(s - lse[:, None]), jnp.float32(0.0))

            def outputs(b, acc):
                def work(a):
                    v_block = lax.dynamic_slice_in_dim(v_all, (b * span).astype(jnp.int32), span, 0)
                    return a + jnp.dot(probs_at(b).astype(jnp.bfloat16), v_block, preferred_element_type=jnp.float32)
                return lax.cond(needed(b), work, lambda a: a, acc)

            out = lax.fori_loop(0, n_blocks, outputs, jnp.zeros((rows, HD), jnp.float32)).astype(jnp.bfloat16)
            delta = jnp.sum(g_rows.astype(jnp.float32) * out.astype(jnp.float32), axis=1)

            def grads(b, state):
                def work(st):
                    dq, dka, dva = st
                    k_start = (b * span).astype(jnp.int32)
                    k_block = lax.dynamic_slice_in_dim(k_all, k_start, span, 0)
                    v_block = lax.dynamic_slice_in_dim(v_all, k_start, span, 0)
                    probs = probs_at(b)
                    dv = lax.dot_general(probs.astype(jnp.bfloat16), g_rows, (((0,), (0,)), ((), ())), preferred_element_type=jnp.float32)
                    dp = lax.dot_general(g_rows, v_block, (((1,), (1,)), ((), ())), preferred_element_type=jnp.float32)
                    ds = (probs * (dp - delta[:, None])).astype(jnp.bfloat16)
                    dq = dq + jnp.dot(ds, k_block, preferred_element_type=jnp.float32) * scale
                    dk = lax.dot_general(ds, q_rows, (((0,), (0,)), ((), ())), preferred_element_type=jnp.float32) * scale
                    zero = jnp.zeros((), jnp.int32)
                    dka = lax.dynamic_update_slice(dka, lax.dynamic_slice_in_dim(dka, k_start, span, 0) + dk, (k_start, zero))
                    dva = lax.dynamic_update_slice(dva, lax.dynamic_slice_in_dim(dva, k_start, span, 0) + dv, (k_start, zero))
                    return dq, dka, dva
                return lax.cond(needed(b), work, lambda st: st, state)

            dq, dk_acc, dv_acc = lax.fori_loop(0, n_blocks, grads, (jnp.zeros((rows, HD), jnp.float32), dk_acc, dv_acc))
            return (dk_acc, dv_acc), (out, dq)

        init = (jnp.zeros((TOKENS, HD), jnp.float32), jnp.zeros((TOKENS, HD), jnp.float32))
        (dk_acc, dv_acc), (outs, dqs) = lax.scan(query_block, init, jnp.arange(n_blocks, dtype=jnp.int32))
        return outs.reshape(TOKENS * group, HD), dqs.reshape(TOKENS * group, HD), dk_acc, dv_acc

    outs, dqs, dks, dvs = lax.map(one_head, (q_heads, g_heads, k_heads, v_heads))
    attn = outs.reshape(KV_HEADS, TOKENS, group, HD).transpose(1, 0, 2, 3).reshape(TOKENS, HEADS * HD)
    mixed = jnp.dot(attn, w_flat, preferred_element_type=jnp.float32).astype(jnp.bfloat16)
    d_queries = dqs.reshape(KV_HEADS, TOKENS, group, HD).transpose(1, 0, 2, 3).reshape(TOKENS, HEADS, HD).astype(jnp.bfloat16)
    d_keys = dks.transpose(1, 0, 2).astype(jnp.bfloat16)
    d_values = dvs.transpose(1, 0, 2).astype(jnp.bfloat16)
    return (mixed, d_queries, d_keys, d_values)
```

```python
import functools

import jax
import jax.numpy as jnp
from jax import lax
from jax.experimental import pallas as pl
from jax.experimental.pallas import tpu as pltpu
from jax.sharding import PartitionSpec as P

NEG_FILL = -1e30
LOG2E = 1.4426950408889634
CTX = ("outer", "inner")
F32 = jnp.float32
BF16 = jnp.bfloat16


def dot_nt(a, b):
    return lax.dot_general(a, b, (((1,), (1,)), ((), ())), preferred_element_type=F32)


def dot_nn(a, b):
    return jnp.dot(a, b, preferred_element_type=F32)


def layout_of(len_ref, me, tok):
    offset = me * tok
    q_pos = offset + lax.broadcasted_iota(jnp.int32, (1, tok), 1)
    begin = jnp.zeros((1, tok), jnp.int32)
    first = jnp.int32(0)
    end = jnp.int32(0)
    for j in range(len_ref.shape[0]):
        end = end + len_ref[j]
        begin = jnp.where(q_pos >= end, end, begin)
        first = jnp.where(offset >= end, end, first)
    n_blocks = me - first // tok + 1
    return q_pos, begin, n_blocks


def bias_of(q_pos, begin, k_start, tok):
    k_pos = k_start + lax.broadcasted_iota(jnp.int32, (tok, tok), 0)
    return jnp.where((k_pos >= begin) & (k_pos <= q_pos), 0.0, NEG_FILL).astype(F32)


def forward_kernel(
    n_kv, heads, scale, len_ref, q_ref, *refs
):
    kv_refs = refs[:n_kv]
    own_ref, pair_ref, w_hbm = refs[n_kv : n_kv + 3]
    far_send, far_keep, near_send, near_keep, attn_ref, lse_ref, d_attn_ref = refs[n_kv + 3 : n_kv + 10]
    kvs, acc, top, denom, rows, w_vmem, w_sem = refs[n_kv + 10 :]
    tok = q_ref.shape[0]
    hd = q_ref.shape[1] // heads
    me = lax.axis_index(CTX)
    t = lax.axis_index("tensor")
    w_copy = pltpu.make_async_copy(w_hbm, w_vmem, w_sem)
    w_copy.start()
    q_pos, begin, n_blocks = layout_of(len_ref, me, tok)
    for d in range(n_kv):

        @pl.when(d < n_blocks)
        def _():
            kvs[d] = kv_refs[d][...]

    top[...] = jnp.full(top.shape, NEG_FILL, F32)
    denom[...] = jnp.zeros(denom.shape, F32)
    acc[...] = jnp.zeros(acc.shape, F32)

    def block(d, carry):
        k = kvs[d, :, :hd]
        v_t = kvs[d, :, hd:].T
        bias = bias_of(q_pos, begin, (me - d) * tok, tok)
        for h in range(heads):
            s = dot_nt(k, q_ref[:, h * hd : (h + 1) * hd]) * (scale * LOG2E) + bias
            old = top[h : h + 1, :]
            new = jnp.maximum(old, jnp.max(s, axis=0, keepdims=True))
            p = jnp.exp2(s - new)
            shrink = jnp.exp2(old - new)
            top[h : h + 1, :] = new
            denom[h : h + 1, :] = denom[h : h + 1, :] * shrink + jnp.sum(p, axis=0, keepdims=True)
            part = slice(h * hd, (h + 1) * hd)
            acc[part, :] = acc[part, :] * shrink + dot_nn(v_t, p.astype(BF16))
        return carry

    lax.fori_loop(0, n_blocks, block, 0)
    lse_ref[...] = top[...] + jnp.log(denom[...]) * LOG2E
    for h in range(heads):
        part = slice(h * hd, (h + 1) * hd)
        out = acc[part, :] / denom[h : h + 1, :]
        attn_ref[:, part] = out.T.astype(BF16)
    quarter = tok // 4
    for i, mask in enumerate((3, 2, 1, 0)):
        rows[i * quarter : (i + 1) * quarter, :] = attn_ref[pl.ds(pl.multiple_of((t ^ mask) * quarter, quarter), quarter), :]
    w_copy.wait()
    width = w_vmem.shape[1]
    step = 512
    for n in range(width // step):
        cols = slice(n * step, (n + 1) * step)
        mixed = dot_nn(rows[...], w_vmem[:, cols]).astype(BF16)
        for i, ref in enumerate((far_send, far_keep, near_send, near_keep)):
            ref[:, cols] = mixed[i * quarter : (i + 1) * quarter, :]
    core = t & 1
    d_attn_ref[pl.ds(pl.multiple_of(core * quarter, quarter), quarter), :] = dot_nt(own_ref[...], w_vmem[...]).astype(BF16)
    d_attn_ref[pl.ds(pl.multiple_of((1 - core) * quarter, quarter), quarter), :] = dot_nt(
        pair_ref[...], w_vmem[...]
    ).astype(BF16)


def backward_kernel(n_kv, heads, scale, len_ref, q_ref, *refs):
    kv_refs = refs[:n_kv]
    attn_ref, lse_ref, near_ref, cross_ref, diag_ref, w_hbm = refs[n_kv : n_kv + 6]
    dq_ref = refs[n_kv + 6]
    out_refs = refs[n_kv + 7 : 2 * n_kv + 7]
    kvs, terms, dq_t, delta, g, w_vmem, w_sem = refs[2 * n_kv + 7 :]
    tok = q_ref.shape[0]
    hd = q_ref.shape[1] // heads
    me = lax.axis_index(CTX)
    t = lax.axis_index("tensor")
    w_copy = pltpu.make_async_copy(w_hbm, w_vmem, w_sem)
    w_copy.start()
    q_pos, begin, n_blocks = layout_of(len_ref, me, tok)
    for d in range(n_kv):

        @pl.when(d < n_blocks)
        def _():
            kvs[d] = kv_refs[d][...]

    quarter = tok // 4
    half = tok // 2
    chip = t >> 1
    g[pl.ds(pl.multiple_of(chip * half, half), half), :] = near_ref[...]
    w_copy.wait()
    for mask, ref in ((2, cross_ref), (3, diag_ref)):
        g[pl.ds(pl.multiple_of((t ^ mask) * quarter, quarter), quarter), :] = dot_nt(ref[...], w_vmem[...]).astype(BF16)
    for h in range(heads):
        part = slice(h * hd, (h + 1) * hd)
        prod = g[:, part].astype(F32) * attn_ref[:, part].astype(F32)
        delta[h : h + 1, :] = jnp.sum(prod.T, axis=0, keepdims=True)
    dq_t[...] = jnp.zeros(dq_t.shape, F32)

    def block(d, carry):
        k = kvs[d, :, :hd]
        v = kvs[d, :, hd:]
        k_t = k.T
        bias = bias_of(q_pos, begin, (me - d) * tok, tok)
        dk = jnp.zeros((tok, hd), F32)
        dv = jnp.zeros((tok, hd), F32)
        for h in range(heads):
            part = slice(h * hd, (h + 1) * hd)
            q = q_ref[:, part]
            g_h = g[:, part]
            s = dot_nt(k, q) * (scale * LOG2E) + bias
            p = jnp.exp2(s - lse_ref[h : h + 1, :])
            dp = dot_nt(v, g_h)
            ds = (p * (dp - delta[h : h + 1, :])).astype(BF16)
            dv = dv + dot_nn(p.astype(BF16), g_h)
            dk = dk + dot_nn(ds, q)
            dq_t[part, :] = dq_t[part, :] + dot_nn(k_t, ds)
        terms[d, :, :hd] = dk * scale
        terms[d, :, hd:] = dv
        return carry

    lax.fori_loop(0, n_blocks, block, 0)
    out_refs[0][...] = terms[0]
    for d in range(1, n_kv):

        @pl.when(d < n_blocks)
        def _():
            out_refs[d][...] = terms[d].astype(BF16)

        @pl.when(d >= n_blocks)
        def _():
            out_refs[d][...] = jnp.zeros(out_refs[d].shape, BF16)

    for h in range(heads):
        part = slice(h * hd, (h + 1) * hd)
        dq_ref[:, part] = (dq_t[part, :] * scale).T.astype(BF16)


def local(queries, keys, values, w_out, d_out, lengths):
    tok, heads, hd = queries.shape
    width = w_out.shape[2]
    ctx = lax.axis_size(CTX)
    longest = tok * ctx * 5 // 8
    reach = min(ctx - 1, -(-(longest - 1) // tok))
    n_kv = reach + 1
    scale = hd ** (-0.5)
    quarter = tok // 4
    n_tensor = lax.axis_size("tensor")

    def swap(x, mask):
        return lax.ppermute(x, "tensor", [(i, i ^ mask) for i in range(n_tensor)])

    def shift(x, d):
        pairs = [(i, i + d) for i in range(ctx - d)] if d > 0 else [(i - d, i) for i in range(ctx + d)]
        return lax.ppermute(x, CTX, pairs)

    q = queries.reshape(tok, heads * hd)
    kv = jnp.concatenate([keys.reshape(tok, hd), values.reshape(tok, hd)], axis=1)
    cross = swap(d_out, 2)
    pair = swap(d_out, 1)
    kvs = [kv] + [shift(kv, d) for d in range(1, n_kv)]
    diag = swap(cross, 1)
    w = w_out.reshape(heads * hd, width)

    vmem = pl.BlockSpec(memory_space=pltpu.VMEM)
    smem = pl.BlockSpec(memory_space=pltpu.SMEM)
    hbm = pl.BlockSpec(memory_space=pl.ANY)
    row = jax.ShapeDtypeStruct((quarter, width), BF16)
    far_send, far_keep, near_send, near_keep, attn, lse, d_near = pl.pallas_call(
        functools.partial(forward_kernel, n_kv, heads, scale),
        out_shape=(
            row,
            row,
            row,
            row,
            jax.ShapeDtypeStruct((tok, heads * hd), BF16),
            jax.ShapeDtypeStruct((heads, tok), F32),
            jax.ShapeDtypeStruct((tok // 2, heads * hd), BF16),
        ),
        in_specs=[smem] + [vmem] * (n_kv + 3) + [hbm],
        out_specs=(vmem,) * 7,
        scratch_shapes=[
            pltpu.VMEM((n_kv, tok, 2 * hd), BF16),
            pltpu.VMEM((heads * hd, tok), F32),
            pltpu.VMEM((heads, tok), F32),
            pltpu.VMEM((heads, tok), F32),
            pltpu.VMEM((tok, heads * hd), BF16),
            pltpu.VMEM((heads * hd, width), BF16),
            pltpu.SemaphoreType.DMA(()),
        ],
        compiler_params=pltpu.CompilerParams(vmem_limit_bytes=40 * 2**20),
        name="forward",
    )(lengths, q, *kvs, d_out, pair, w)

    from_pair = swap(far_send, 1)
    to_cross = (from_pair.astype(F32) + far_keep.astype(F32)).astype(BF16)
    from_cross = swap(to_cross, 2)
    near_pair = swap(near_send, 1)

    dq, *terms = pl.pallas_call(
        functools.partial(backward_kernel, n_kv, heads, scale),
        out_shape=(
            jax.ShapeDtypeStruct((tok, heads * hd), BF16),
            jax.ShapeDtypeStruct((tok, 2 * hd), F32),
        )
        + (jax.ShapeDtypeStruct((tok, 2 * hd), BF16),) * reach,
        in_specs=[smem] + [vmem] * (n_kv + 6) + [hbm],
        out_specs=(vmem,) * (n_kv + 1),
        scratch_shapes=[
            pltpu.VMEM((n_kv, tok, 2 * hd), BF16),
            pltpu.VMEM((n_kv, tok, 2 * hd), F32),
            pltpu.VMEM((heads * hd, tok), F32),
            pltpu.VMEM((heads, tok), F32),
            pltpu.VMEM((tok, heads * hd), BF16),
            pltpu.VMEM((heads * hd, width), BF16),
            pltpu.SemaphoreType.DMA(()),
        ],
        compiler_params=pltpu.CompilerParams(vmem_limit_bytes=48 * 2**20),
        name="backward",
    )(lengths, q, *kvs, attn, lse, d_near, cross, diag, w)

    total = terms[0]
    for d in range(1, n_kv):
        total = total + shift(terms[d], -d).astype(F32)
    mixed = (near_keep.astype(F32) + near_pair.astype(F32) + from_cross.astype(F32)).astype(BF16)
    grads = total.astype(BF16).reshape(tok, 1, 2 * hd)
    return (mixed, dq.reshape(tok, heads, hd), grads[:, :, :hd], grads[:, :, hd:])


def solution(mesh):
    return jax.shard_map(
        local,
        mesh=mesh,
        in_specs=(
            P(("outer", "inner"), "tensor", None),
            P(("outer", "inner"), "tensor", None),
            P(("outer", "inner"), "tensor", None),
            P("tensor", None, None),
            P(("outer", "inner", "tensor"), None),
            P(),
        ),
        out_specs=(
            P(("outer", "inner", "tensor"), None),
            P(("outer", "inner"), "tensor", None),
            P(("outer", "inner"), "tensor", None),
            P(("outer", "inner"), "tensor", None),
        ),
        check_vma=False,
    )
```

```python
import functools

import jax
import jax.numpy as jnp
from jax import lax
from jax.experimental import pallas as pl
from jax.experimental.pallas import tpu as pltpu
from jax.sharding import PartitionSpec as P

NEG_FILL = -1e30
LOG2E = 1.4426950408889634
CTX = ("outer", "inner")
F32 = jnp.float32
BF16 = jnp.bfloat16


def dot_nt(a, b):
    return lax.dot_general(a, b, (((1,), (1,)), ((), ())), preferred_element_type=F32)


def dot_nn(a, b):
    return jnp.dot(a, b, preferred_element_type=F32)


def layout_of(len_ref, me, tok):
    offset = me * tok
    q_pos = offset + lax.broadcasted_iota(jnp.int32, (1, tok), 1)
    begin = jnp.zeros((1, tok), jnp.int32)
    first = jnp.int32(0)
    end = jnp.int32(0)
    for j in range(len_ref.shape[0]):
        end = end + len_ref[j]
        begin = jnp.where(q_pos >= end, end, begin)
        first = jnp.where(offset >= end, end, first)
    n_blocks = me - first // tok + 1
    return q_pos, begin, n_blocks


def bias_of(q_pos, begin, k_start, tok):
    k_pos = k_start + lax.broadcasted_iota(jnp.int32, (tok, tok), 0)
    return jnp.where((k_pos >= begin) & (k_pos <= q_pos), 0.0, NEG_FILL).astype(F32)


def stage(kvs, kv_refs, n_blocks):
    for d, ref in enumerate(kv_refs):

        @pl.when(d < n_blocks)
        def _():
            kvs[d] = ref[...]


def d_attn_kernel(own_hbm, pair_hbm, w_hbm, out_ref, w_ref, rows, total, sems):
    core = lax.axis_index("tensor") & 1
    quarter = own_hbm.shape[0]
    width = w_ref.shape[1]
    steps = sems.shape[0] - 2
    step = width // steps
    copies = [
        pltpu.make_async_copy(own_hbm, rows.at[pl.ds(pl.multiple_of(core * quarter, quarter), quarter), :], sems.at[0]),
        pltpu.make_async_copy(
            pair_hbm, rows.at[pl.ds(pl.multiple_of((1 - core) * quarter, quarter), quarter), :], sems.at[1]
        ),
    ]
    for i in range(steps):
        cols = slice(i * step, (i + 1) * step)
        copies.append(pltpu.make_async_copy(w_hbm.at[:, cols], w_ref.at[:, cols], sems.at[2 + i]))
    for copy in copies:
        copy.start()
    copies[0].wait()
    copies[1].wait()
    for i in range(steps):
        cols = slice(i * step, (i + 1) * step)
        copies[2 + i].wait()
        part = dot_nt(rows[:, cols], w_ref[:, cols])
        total[...] = part if i == 0 else total[...] + part
    out_ref[...] = total[...].astype(BF16)


def by_head(ref, out, tok, hd):
    for h in range(ref.shape[1] // hd):
        out[h * tok : (h + 1) * tok, :] = ref[:, h * hd : (h + 1) * hd]


def forward_kernel(lo, n_kv, heads, scale, len_ref, q_ref, *refs):
    kv_refs = refs[:n_kv]
    refs = refs[n_kv:]
    if lo == 0:
        top, denom, acc, kvs, qs = refs
    else:
        top_in, denom_in, acc_in, attn_ref, lse_ref, kvs, qs, top, denom, acc = refs
    tok = q_ref.shape[0]
    hd = q_ref.shape[1] // heads
    me = lax.axis_index(CTX)
    q_pos, begin, n_blocks = layout_of(len_ref, me, tok)
    n_here = jnp.clip(n_blocks - lo, 0, n_kv)
    stage(kvs, kv_refs, n_here)
    by_head(q_ref, qs, tok, hd)
    if lo == 0:
        top[...] = jnp.full(top.shape, NEG_FILL, F32)
        denom[...] = jnp.zeros(denom.shape, F32)
        acc[...] = jnp.zeros(acc.shape, F32)
    else:
        top[...] = top_in[...]
        denom[...] = denom_in[...]
        acc[...] = acc_in[...]

    def block(d, carry):
        k = kvs[d, :, :hd]
        v_t = kvs[d, :, hd:].T
        bias = bias_of(q_pos, begin, (me - lo - d) * tok, tok)
        s = dot_nt(k, qs[...]) * (scale * LOG2E) + jnp.concatenate([bias] * heads, axis=1)
        old = top[...]
        new = jnp.maximum(old, jnp.max(s, axis=0, keepdims=True))
        p = jnp.exp2(s - new)
        shrink = jnp.exp2(old - new)
        top[...] = new
        denom[...] = denom[...] * shrink + jnp.sum(p, axis=0, keepdims=True)
        acc[...] = acc[...] * shrink + dot_nn(v_t, p.astype(BF16))
        return carry

    lax.fori_loop(0, n_here, block, 0)
    if lo == 0:
        return
    lse_ref[...] = top[...] + jnp.log(denom[...]) * LOG2E
    for h in range(heads):
        cols = slice(h * tok, (h + 1) * tok)
        attn_ref[:, h * hd : (h + 1) * hd] = (acc[:, cols] / denom[:, cols]).T.astype(BF16)


def middle_kernel(heads, attn_ref, near_ref, cross_ref, diag_ref, w_ref, *refs):
    send_ref, keep_ref, g_ref, delta_ref, rows, others = refs
    t = lax.axis_index("tensor")
    chip, core = t >> 1, t & 1
    tok = attn_ref.shape[0]
    hd = attn_ref.shape[1] // heads
    quarter, half = tok // 4, tok // 2
    for i, mask in enumerate((3, 1, 2, 0)):
        rows[i * quarter : (i + 1) * quarter, :] = attn_ref[pl.ds(pl.multiple_of((t ^ mask) * quarter, quarter), quarter), :]
    width = w_ref.shape[1]
    step = 512
    for n in range(width // step):
        cols = slice(n * step, (n + 1) * step)
        mixed = dot_nn(rows[...], w_ref[:, cols]).astype(BF16)
        send_ref[:, cols] = mixed[:half, :]
        keep_ref[:, cols] = mixed[half:, :]
    others[pl.ds(pl.multiple_of(core * quarter, quarter), quarter), :] = cross_ref[...]
    others[pl.ds(pl.multiple_of((1 - core) * quarter, quarter), quarter), :] = diag_ref[...]
    g_ref[pl.ds(pl.multiple_of(chip * half, half), half), :] = near_ref[...]
    g_ref[pl.ds(pl.multiple_of((1 - chip) * half, half), half), :] = dot_nt(others[...], w_ref[...]).astype(BF16)
    for h in range(heads):
        part = slice(h * hd, (h + 1) * hd)
        prod = g_ref[:, part].astype(F32) * attn_ref[:, part].astype(F32)
        delta_ref[:, h * tok : (h + 1) * tok] = jnp.sum(prod.T, axis=0, keepdims=True)


def backward_kernel(lo, n_kv, heads, scale, len_ref, q_ref, *refs):
    kv_refs = refs[:n_kv]
    refs = refs[n_kv:]
    if lo == 0:
        g_ref, lse_ref, delta_ref, dq_in = refs[:4]
        dq_ref = refs[4]
        refs = refs[5:]
    else:
        g_ref, lse_ref, delta_ref = refs[:3]
        dq_out = refs[3]
        refs = refs[4:]
    out_refs = refs[:n_kv]
    kvs, terms, qs, gs = refs[n_kv : n_kv + 4]
    dq_t = refs[n_kv + 4] if lo == 0 else dq_out
    tok = q_ref.shape[0]
    hd = q_ref.shape[1] // heads
    me = lax.axis_index(CTX)
    q_pos, begin, n_blocks = layout_of(len_ref, me, tok)
    n_here = jnp.clip(n_blocks - lo, 0, n_kv)
    stage(kvs, kv_refs, n_here)
    by_head(q_ref, qs, tok, hd)
    by_head(g_ref, gs, tok, hd)
    dq_t[...] = dq_in[...] if lo == 0 else jnp.zeros(dq_t.shape, F32)

    def block(d, carry):
        k = kvs[d, :, :hd]
        bias = bias_of(q_pos, begin, (me - lo - d) * tok, tok)
        s = dot_nt(k, qs[...]) * (scale * LOG2E) + jnp.concatenate([bias] * heads, axis=1)
        p = jnp.exp2(s - lse_ref[...])
        dp = dot_nt(kvs[d, :, hd:], gs[...])
        ds = (p * (dp - delta_ref[...])).astype(BF16)
        terms[d, :, :hd] = (dot_nn(ds, qs[...]) * scale).astype(terms.dtype)
        terms[d, :, hd:] = dot_nn(p.astype(BF16), gs[...]).astype(terms.dtype)
        dq_t[...] = dq_t[...] + dot_nn(k.T, ds)
        return carry

    lax.fori_loop(0, n_here, block, 0)
    for d in range(n_kv):

        @pl.when(d < n_here)
        def _():
            out_refs[d][...] = terms[d].astype(out_refs[d].dtype)

        @pl.when(d >= n_here)
        def _():
            out_refs[d][...] = jnp.zeros(out_refs[d].shape, out_refs[d].dtype)

    if lo == 0:
        for h in range(heads):
            dq_ref[:, h * hd : (h + 1) * hd] = (dq_t[:, h * tok : (h + 1) * tok] * scale).T.astype(BF16)


def finish_kernel(*refs):
    dk_ref, dv_ref = refs[-2:]
    total = refs[0][...]
    for ref in refs[1:-2]:
        total = total + ref[...].astype(F32)
    hd = dk_ref.shape[1]
    dk_ref[...] = total[:, :hd].astype(BF16)
    dv_ref[...] = total[:, hd:].astype(BF16)


def pair_sum_kernel(keep_ref, pair_ref, out_ref):
    n = out_ref.shape[0]
    out_ref[...] = (keep_ref[:n, :].astype(F32) + pair_ref[:n, :].astype(F32)).astype(BF16)


def mixed_sum_kernel(keep_ref, pair_ref, cross_ref, out_ref):
    n = out_ref.shape[0]
    total = keep_ref[n:, :].astype(F32) + pair_ref[n:, :].astype(F32) + cross_ref[...].astype(F32)
    out_ref[...] = total.astype(BF16)


def call(kernel, name, out_shape, args, scratch=(), smem=0, hbm=0, us=1.0):
    vmem = pl.BlockSpec(memory_space=pltpu.VMEM)
    return pl.pallas_call(
        kernel,
        out_shape=out_shape,
        in_specs=[pl.BlockSpec(memory_space=pltpu.SMEM)] * smem
        + [pl.BlockSpec(memory_space=pl.ANY)] * hbm
        + [vmem] * (len(args) - smem - hbm),
        out_specs=jax.tree.map(lambda _: vmem, out_shape),
        scratch_shapes=list(scratch),
        compiler_params=pltpu.CompilerParams(vmem_limit_bytes=24 * 2**20),
        cost_estimate=pl.CostEstimate(flops=int(us * 1e9), bytes_accessed=int(us * 3e6), transcendentals=0),
        name=name,
    )(*args)


def local(queries, keys, values, w_out, d_out, lengths):
    tok, heads, hd = queries.shape
    width = w_out.shape[2]
    ctx = lax.axis_size(CTX)
    longest = tok * ctx * 5 // 8
    reach = min(ctx - 1, -(-(longest - 1) // tok))
    n_kv = reach + 1
    split = (n_kv + 1) // 2
    scale = hd ** (-0.5)
    quarter = tok // 4
    n_tensor = lax.axis_size("tensor")
    shape = jax.ShapeDtypeStruct

    def swap(x, mask):
        return lax.ppermute(x, "tensor", [(i, i ^ mask) for i in range(n_tensor)])

    def shift(x, d):
        pairs = [(i, i + d) for i in range(ctx - d)] if d > 0 else [(i - d, i) for i in range(ctx + d)]
        return lax.ppermute(x, CTX, pairs)

    q = queries.reshape(tok, heads * hd)
    kv = jnp.concatenate([keys.reshape(tok, hd), values.reshape(tok, hd)], axis=1)
    w = w_out.reshape(heads * hd, width)
    pair = swap(d_out, 1)
    cross = swap(d_out, 2)
    kv, pair = lax.optimization_barrier((kv, pair))
    kvs = [kv] + [shift(kv, d) for d in range(1, n_kv)]
    half_rows = pltpu.VMEM((tok // 2, width), BF16)
    d_near, w = call(
        d_attn_kernel,
        "d_attn_near",
        (shape((tok // 2, heads * hd), BF16), shape((heads * hd, width), BF16)),
        (d_out, pair, w),
        scratch=(half_rows, pltpu.VMEM((tok // 2, heads * hd), F32), pltpu.SemaphoreType.DMA((10,))),
        hbm=3,
        us=2.0,
    )
    row = shape((1, heads * tok), F32)
    state = (row, row, shape((hd, heads * tok), F32))
    all_rows = pltpu.VMEM((heads * tok, hd), BF16)
    begun = call(
        functools.partial(forward_kernel, 0, split, heads, scale),
        "forward_near",
        state,
        (lengths, q, *kvs[:split]),
        scratch=(pltpu.VMEM((split, tok, 2 * hd), BF16), all_rows),
        smem=1,
        us=4.0,
    )
    attn, lse = call(
        functools.partial(forward_kernel, split, n_kv - split, heads, scale),
        "forward_far",
        (shape((tok, heads * hd), BF16), row),
        (lengths, q, *kvs[split:], *begun),
        scratch=(pltpu.VMEM((n_kv - split, tok, 2 * hd), BF16), all_rows)
        + tuple(pltpu.VMEM(x.shape, F32) for x in state),
        smem=1,
        us=4.0,
    )
    cross, *rest = lax.optimization_barrier((cross, *kvs[1:], d_near))
    d_near = rest[-1]
    diag = swap(cross, 1)
    send, keep, g, delta = call(
        functools.partial(middle_kernel, heads),
        "middle",
        (shape((tok // 2, width), BF16),) * 2 + (shape((tok, heads * hd), BF16), row),
        (attn, d_near, cross, diag, w),
        scratch=(pltpu.VMEM((tok, heads * hd), BF16), half_rows),
        us=3.0,
    )
    from_pair = swap(send, 1)

    def backward(lo, hi, extra):
        n = hi - lo
        dq_shape = shape((tok, heads * hd), BF16) if lo == 0 else state[2]
        outs = tuple(shape((tok, 2 * hd), F32 if lo + i == 0 else BF16) for i in range(n))
        scratch = [pltpu.VMEM((n, tok, 2 * hd), BF16), pltpu.VMEM((n, tok, 2 * hd), F32 if lo == 0 else BF16)]
        scratch += [all_rows, all_rows]
        if lo == 0:
            scratch.append(pltpu.VMEM(state[2].shape, F32))
        dq, *terms = call(
            functools.partial(backward_kernel, lo, n, heads, scale),
            "backward_near" if lo == 0 else "backward_far",
            (dq_shape,) + outs,
            (lengths, q, *kvs[lo:hi], g, lse, delta) + extra,
            scratch=scratch,
            smem=1,
            us=4.0,
        )
        return dq, terms

    dq_t, far_terms = backward(split, n_kv, ())
    to_cross = call(pair_sum_kernel, "pair_sum", shape((quarter, width), BF16), (keep, from_pair), us=0.5)
    from_cross = swap(to_cross, 2)
    far_back = [shift(x, -(split + i)) for i, x in enumerate(far_terms)]
    dq_t, to_cross = lax.optimization_barrier((dq_t, to_cross))
    dq, near_terms = backward(0, split, (dq_t,))
    near_back = [shift(x, -i) for i, x in enumerate(near_terms) if i > 0]
    mixed = call(mixed_sum_kernel, "mixed_sum", shape((quarter, width), BF16), (keep, from_pair, from_cross), us=0.5)
    own, mixed = lax.optimization_barrier((near_terms[0], mixed))
    dk, dv = call(
        finish_kernel,
        "finish",
        (shape((tok, hd), BF16),) * 2,
        (own, *far_back, *near_back),
        us=0.5,
    )
    return (mixed, dq.reshape(tok, heads, hd), dk.reshape(tok, 1, hd), dv.reshape(tok, 1, hd))


def solution(mesh):
    return jax.shard_map(
        local,
        mesh=mesh,
        in_specs=(
            P(("outer", "inner"), "tensor", None),
            P(("outer", "inner"), "tensor", None),
            P(("outer", "inner"), "tensor", None),
            P("tensor", None, None),
            P(("outer", "inner", "tensor"), None),
            P(),
        ),
        out_specs=(
            P(("outer", "inner", "tensor"), None),
            P(("outer", "inner"), "tensor", None),
            P(("outer", "inner"), "tensor", None),
            P(("outer", "inner"), "tensor", None),
        ),
        check_vma=False,
    )
```

```python
import functools

import jax
import jax.numpy as jnp
from jax import lax
from jax.experimental import pallas as pl
from jax.experimental.pallas import tpu as pltpu
from jax.sharding import PartitionSpec as P

NEG_FILL = -1e30
LOG2E = 1.4426950408889634
CTX = ("outer", "inner")
F32 = jnp.float32
BF16 = jnp.bfloat16


def dot_nt(a, b):
    return lax.dot_general(a, b, (((1,), (1,)), ((), ())), preferred_element_type=F32)


def dot_nn(a, b):
    return jnp.dot(a, b, preferred_element_type=F32)


def layout_of(len_ref, me, tok):
    offset = me * tok
    q_pos = offset + lax.broadcasted_iota(jnp.int32, (1, tok), 1)
    begin = jnp.zeros((1, tok), jnp.int32)
    first = jnp.int32(0)
    end = jnp.int32(0)
    for j in range(len_ref.shape[0]):
        end = end + len_ref[j]
        begin = jnp.where(q_pos >= end, end, begin)
        first = jnp.where(offset >= end, end, first)
    n_blocks = me - first // tok + 1
    return q_pos, begin, n_blocks


def bias_of(q_pos, begin, k_start, tok):
    k_pos = k_start + lax.broadcasted_iota(jnp.int32, (tok, tok), 0)
    return jnp.where((k_pos >= begin) & (k_pos <= q_pos), 0.0, NEG_FILL).astype(F32)


UNROLL = 8


def each_block(blocks, kv_refs, held, n_blocks, work):
    if len(blocks) <= UNROLL:
        for i, d in enumerate(blocks):

            @pl.when(d < n_blocks)
            def _():
                work(i, d, kv_refs[i])

        return
    for i, d in enumerate(blocks):

        @pl.when(d < n_blocks)
        def _():
            held[i] = kv_refs[i][...]

    def step(i, carry):
        work(i, blocks[0] + i, held.at[i])
        return carry

    lax.fori_loop(0, jnp.clip(n_blocks - blocks[0], 0, len(blocks)), step, 0)


def begin_kernel(len_ref, out_ref):
    tok = out_ref.shape[1]
    _, begin, _ = layout_of(len_ref, lax.axis_index(CTX), tok)
    out_ref[...] = begin


def d_attn_kernel(own_ref, pair_ref, w_ref, out_ref, rows):
    core = lax.axis_index("tensor") & 1
    quarter = own_ref.shape[0]
    rows[pl.ds(pl.multiple_of(core * quarter, quarter), quarter), :] = own_ref[...]
    rows[pl.ds(pl.multiple_of((1 - core) * quarter, quarter), quarter), :] = pair_ref[...]
    out_ref[...] = dot_nt(rows[...], w_ref[...]).astype(BF16)


def forward_kernel(blocks, heads, scale, len_ref, begin_ref, q_ref, *refs):
    n = len(blocks)
    kv_refs = refs[:n]
    if blocks[0] == 0:
        top, denom, acc, held = refs[n:]
    else:
        top_in, denom_in, acc_in, attn_ref, lse_ref, held, top, denom, acc = refs[n:]
    tok, hd = q_ref.shape[0] // heads, q_ref.shape[1]
    me = lax.axis_index(CTX)
    q_pos, _, n_blocks = layout_of(len_ref, me, tok)
    begin = begin_ref[...]
    if blocks[0] == 0:
        top[...] = jnp.full(top.shape, NEG_FILL, F32)
        denom[...] = jnp.zeros(denom.shape, F32)
        acc[...] = jnp.zeros(acc.shape, F32)
    else:
        top[...] = top_in[...]
        denom[...] = denom_in[...]
        acc[...] = acc_in[...]

    def work(i, d, kv):
        v_t = kv[:, hd:].T
        bias = bias_of(q_pos, begin, (me - d) * tok, tok)
        s = dot_nt(kv[:, :hd], q_ref[...]) * (scale * LOG2E) + jnp.concatenate([bias] * heads, axis=1)
        old = top[...]
        new = jnp.maximum(old, jnp.max(s, axis=0, keepdims=True))
        p = jnp.exp2(s - new)
        shrink = jnp.exp2(old - new)
        top[...] = new
        denom[...] = denom[...] * shrink + jnp.sum(p, axis=0, keepdims=True)
        acc[...] = acc[...] * shrink + dot_nn(v_t, p.astype(BF16))

    each_block(blocks, kv_refs, held, n_blocks, work)
    if blocks[0] == 0:
        return
    lse_ref[...] = top[...] + jnp.log(denom[...]) * LOG2E
    for h in range(heads):
        cols = slice(h * tok, (h + 1) * tok)
        attn_ref[:, h * hd : (h + 1) * hd] = (acc[:, cols] / denom[:, cols]).T.astype(BF16)


def middle_kernel(heads, attn_ref, near_ref, cross_ref, diag_ref, w_ref, *refs):
    send_ref, keep_ref, g_ref, delta_ref, rows, others = refs
    t = lax.axis_index("tensor")
    chip, core = t >> 1, t & 1
    tok = attn_ref.shape[0]
    hd = attn_ref.shape[1] // heads
    quarter, half = tok // 4, tok // 2
    for i, mask in enumerate((3, 1, 2, 0)):
        rows[i * quarter : (i + 1) * quarter, :] = attn_ref[pl.ds(pl.multiple_of((t ^ mask) * quarter, quarter), quarter), :]
    width = w_ref.shape[1]
    step = 512
    for n in range(width // step):
        cols = slice(n * step, (n + 1) * step)
        mixed = dot_nn(rows[...], w_ref[:, cols]).astype(BF16)
        send_ref[:, cols] = mixed[:half, :]
        keep_ref[:, cols] = mixed[half:, :]
    others[pl.ds(pl.multiple_of(core * quarter, quarter), quarter), :] = cross_ref[...]
    others[pl.ds(pl.multiple_of((1 - core) * quarter, quarter), quarter), :] = diag_ref[...]
    far = dot_nt(others[...], w_ref[...]).astype(BF16)
    for h in range(heads):
        part = slice(h * hd, (h + 1) * hd)
        g_ref[pl.ds(pl.multiple_of(h * tok + chip * half, half), half), :] = near_ref[:, part]
        g_ref[pl.ds(pl.multiple_of(h * tok + (1 - chip) * half, half), half), :] = far[:, part]
        cols = slice(h * tok, (h + 1) * tok)
        prod = g_ref[cols, :].astype(F32) * attn_ref[:, part].astype(F32)
        delta_ref[:, cols] = jnp.sum(prod.T, axis=0, keepdims=True)


def backward_kernel(blocks, first, last, heads, scale, len_ref, begin_ref, q_ref, *refs):
    n = len(blocks)
    kv_refs = refs[:n]
    g_ref, lse_ref, delta_ref = refs[n : n + 3]
    refs = refs[n + 3 :]
    if not first:
        dq_in, *refs = refs
    if last:
        dq_ref, *refs = refs
    else:
        dq_t, *refs = refs
    out_refs = refs[:n]
    held, terms = refs[n : n + 2]
    if last:
        dq_t = refs[n + 2]
    tok, hd = q_ref.shape[0] // heads, q_ref.shape[1]
    me = lax.axis_index(CTX)
    q_pos, _, n_blocks = layout_of(len_ref, me, tok)
    begin = begin_ref[...]
    dq_t[...] = jnp.zeros(dq_t.shape, F32) if first else dq_in[...]

    def work(i, d, kv):
        k = kv[:, :hd]
        bias = bias_of(q_pos, begin, (me - d) * tok, tok)
        s = dot_nt(k, q_ref[...]) * (scale * LOG2E) + jnp.concatenate([bias] * heads, axis=1)
        p = jnp.exp2(s - lse_ref[...])
        dp = dot_nt(kv[:, hd:], g_ref[...])
        ds = (p * (dp - delta_ref[...])).astype(BF16)
        out = out_refs[i] if n <= UNROLL else terms.at[i]
        out[:, :hd] = (dot_nn(ds, q_ref[...]) * scale).astype(BF16)
        out[:, hd:] = dot_nn(p.astype(BF16), g_ref[...]).astype(BF16)
        dq_t[...] = dq_t[...] + dot_nn(k.T, ds)

    each_block(blocks, kv_refs, held, n_blocks, work)
    for i, d in enumerate(blocks):
        if n > UNROLL:

            @pl.when(d < n_blocks)
            def _():
                out_refs[i][...] = terms[i]

        @pl.when(d >= n_blocks)
        def _():
            out_refs[i][...] = jnp.zeros(out_refs[i].shape, BF16)

    if last:
        for h in range(heads):
            dq_ref[:, h * hd : (h + 1) * hd] = (dq_t[:, h * tok : (h + 1) * tok] * scale).T.astype(BF16)


def finish_kernel(n_kv, *refs):
    sources = refs[:n_kv]
    dk_ref, dv_ref, held, sems = refs[n_kv:]
    copies = [pltpu.make_async_copy(ref, held.at[d], sems.at[d]) for d, ref in enumerate(sources)]
    for copy in copies:
        copy.start()
    for copy in copies:
        copy.wait()
    total = held[0].astype(F32)
    for d in range(1, n_kv):
        total = total + held[d].astype(F32)
    hd = dk_ref.shape[1]
    dk_ref[...] = total[:, :hd].astype(BF16)
    dv_ref[...] = total[:, hd:].astype(BF16)


def pair_sum_kernel(keep_ref, pair_ref, out_ref):
    n = out_ref.shape[0]
    out_ref[...] = (keep_ref[:n, :].astype(F32) + pair_ref[:n, :].astype(F32)).astype(BF16)


def mixed_sum_kernel(keep_ref, pair_ref, cross_ref, out_ref):
    n = out_ref.shape[0]
    total = keep_ref[n:, :].astype(F32) + pair_ref[n:, :].astype(F32) + cross_ref[...].astype(F32)
    out_ref[...] = total.astype(BF16)


def call(kernel, name, out_shape, args, scratch=(), smem=0, hbm=0, us=1.0, vmem_mb=24):
    vmem = pl.BlockSpec(memory_space=pltpu.VMEM)
    return pl.pallas_call(
        kernel,
        out_shape=out_shape,
        in_specs=[pl.BlockSpec(memory_space=pltpu.SMEM)] * smem
        + [pl.BlockSpec(memory_space=pltpu.HBM)] * hbm
        + [vmem] * (len(args) - smem - hbm),
        out_specs=jax.tree.map(lambda _: vmem, out_shape),
        scratch_shapes=list(scratch),
        compiler_params=pltpu.CompilerParams(vmem_limit_bytes=vmem_mb * 2**20),
        cost_estimate=pl.CostEstimate(flops=int(us * 1e9), bytes_accessed=0, transcendentals=0),
        name=name,
    )(*args)


def local(queries, keys, values, w_out, d_out, lengths):
    tok, heads, hd = queries.shape
    width = w_out.shape[2]
    ctx = lax.axis_size(CTX)
    longest = tok * ctx * 5 // 8
    reach = min(ctx - 1, -(-(longest - 1) // tok))
    n_kv = reach + 1
    split = min(n_kv, 4)
    scale = hd ** (-0.5)
    quarter = tok // 4
    n_tensor = lax.axis_size("tensor")
    shape = jax.ShapeDtypeStruct

    def swap(x, mask):
        return lax.ppermute(x, "tensor", [(i, i ^ mask) for i in range(n_tensor)])

    def shift(x, d):
        pairs = [(i, i + d) for i in range(ctx - d)] if d > 0 else [(i - d, i) for i in range(ctx + d)]
        return lax.ppermute(x, CTX, pairs)

    begin = call(begin_kernel, "begin", shape((1, tok), jnp.int32), (lengths,), smem=1, us=6.0)
    keys, values, begin = lax.optimization_barrier((keys, values, begin))
    kv = jnp.concatenate([keys.reshape(tok, hd), values.reshape(tok, hd)], axis=1)
    w = w_out.reshape(heads * hd, width)
    pair = swap(d_out, 1)
    cross = swap(d_out, 2)
    kvs = [kv] + [shift(kv, d) for d in range(1, split)]
    kv_later, pair, queries, kvs[1] = lax.optimization_barrier((kv, pair, queries, kvs[1]))
    q = queries.transpose(1, 0, 2).reshape(heads * tok, hd)
    kvs += [shift(kv_later, d) for d in range(split, n_kv)]
    near, far = list(range(split)), list(range(split, n_kv))
    half_rows = pltpu.VMEM((tok // 2, width), BF16)
    d_near = call(
        d_attn_kernel, "d_attn_near", shape((tok // 2, heads * hd), BF16), (d_out, pair, w), scratch=(half_rows,), us=2.0
    )
    q, d_near = lax.optimization_barrier((q, d_near))
    row = shape((1, heads * tok), F32)
    state = (row, row, shape((hd, heads * tok), F32))
    held = pltpu.VMEM((split if split > UNROLL else 1, tok, 2 * hd), BF16)

    def blocks_of(group):
        return tuple(kvs[d] for d in group)

    begun = call(
        functools.partial(forward_kernel, near, heads, scale),
        "forward_near",
        state,
        (lengths, begin, q, *blocks_of(near)),
        scratch=(held,),
        smem=1,
        us=0.2,
    )
    attn, lse = call(
        functools.partial(forward_kernel, far, heads, scale),
        "forward_far",
        (shape((tok, heads * hd), BF16), row),
        (lengths, begin, q, *blocks_of(far), *begun),
        scratch=(held,) + tuple(pltpu.VMEM(x.shape, F32) for x in state),
        smem=1,
        us=5.0,
    )
    diag = swap(cross, 1)
    send, keep, g, delta = call(
        functools.partial(middle_kernel, heads),
        "middle",
        (shape((tok // 2, width), BF16),) * 2 + (shape((heads * tok, hd), BF16), row),
        (attn, d_near, cross, diag, w),
        scratch=(pltpu.VMEM((tok, heads * hd), BF16), half_rows),
        us=3.0,
    )
    from_pair = swap(send, 1)
    term = shape((tok, 2 * hd), BF16)

    def backward(blocks, name, us, dq=None, last=False):
        dq, *terms = call(
            functools.partial(backward_kernel, blocks, dq is None, last, heads, scale),
            name,
            (shape((tok, heads * hd), BF16) if last else state[2],) + (term,) * len(blocks),
            (lengths, begin, q, *blocks_of(blocks), g, lse, delta) + (() if dq is None else (dq,)),
            scratch=(held, held) + ((pltpu.VMEM(state[2].shape, F32),) if last else ()),
            smem=1,
            us=us,
        )
        return dq, dict(zip(blocks, terms))

    dq, terms = backward(near[1:], "backward_near", 3.0)
    from_pair, dq = lax.optimization_barrier((from_pair, dq))
    back = {d: shift(terms[d], -d) for d in reversed(near[1:])}
    to_cross = call(pair_sum_kernel, "pair_sum", shape((quarter, width), BF16), (keep, from_pair), us=0.5)
    from_cross = swap(to_cross, 2)
    dq, to_cross = lax.optimization_barrier((dq, to_cross))
    dq, terms = backward(far, "backward_far", 3.0, dq)
    back.update({d: shift(terms[d], -d) for d in far})
    dq, terms = backward([0], "backward_own", 2.0, dq, True)
    back = [terms[0]] + [back[d] for d in range(1, n_kv)]
    mixed = call(mixed_sum_kernel, "mixed_sum", shape((quarter, width), BF16), (keep, from_pair, from_cross), us=0.5)
    back[0], mixed = lax.optimization_barrier((back[0], mixed))
    dk, dv = call(
        functools.partial(finish_kernel, n_kv),
        "finish",
        (shape((tok, hd), BF16),) * 2,
        tuple(back),
        scratch=(pltpu.VMEM((n_kv, tok, 2 * hd), BF16), pltpu.SemaphoreType.DMA((n_kv,))),
        hbm=n_kv,
        us=0.5,
        vmem_mb=60,
    )
    return (mixed, dq.reshape(tok, heads, hd), dk.reshape(tok, 1, hd), dv.reshape(tok, 1, hd))


def solution(mesh):
    return jax.shard_map(
        local,
        mesh=mesh,
        in_specs=(
            P(("outer", "inner"), "tensor", None),
            P(("outer", "inner"), "tensor", None),
            P(("outer", "inner"), "tensor", None),
            P("tensor", None, None),
            P(("outer", "inner", "tensor"), None),
            P(),
        ),
        out_specs=(
            P(("outer", "inner", "tensor"), None),
            P(("outer", "inner"), "tensor", None),
            P(("outer", "inner"), "tensor", None),
            P(("outer", "inner"), "tensor", None),
        ),
        check_vma=False,
    )
```

```python
import functools

import jax
import jax.numpy as jnp
from jax import lax
from jax.experimental import pallas as pl
from jax.experimental.pallas import tpu as pltpu
from jax.sharding import PartitionSpec as P

NEG_FILL = -1e30
LOG2E = 1.4426950408889634
CTX = ("outer", "inner")
F32 = jnp.float32
BF16 = jnp.bfloat16


def dot_nt(a, b):
    return lax.dot_general(a, b, (((1,), (1,)), ((), ())), preferred_element_type=F32)


def dot_nn(a, b):
    return jnp.dot(a, b, preferred_element_type=F32)


def layout_of(len_ref, me, tok):
    offset = me * tok
    q_pos = offset + lax.broadcasted_iota(jnp.int32, (1, tok), 1)
    begin = jnp.zeros((1, tok), jnp.int32)
    first = jnp.int32(0)
    end = jnp.int32(0)
    for j in range(len_ref.shape[0]):
        end = end + len_ref[j]
        begin = jnp.where(q_pos >= end, end, begin)
        first = jnp.where(offset >= end, end, first)
    n_blocks = me - first // tok + 1
    return q_pos, begin, n_blocks


def bias_of(q_pos, begin, k_start, tok):
    k_pos = k_start + lax.broadcasted_iota(jnp.int32, (tok, tok), 0)
    return jnp.where((k_pos >= begin) & (k_pos <= q_pos), 0.0, NEG_FILL).astype(F32)


UNROLL = 8


def each_block(blocks, kv_refs, held, n_blocks, work):
    if len(blocks) <= UNROLL:
        for i, d in enumerate(blocks):

            @pl.when(d < n_blocks)
            def _():
                work(i, d, kv_refs[i])

        return
    for i, d in enumerate(blocks):

        @pl.when(d < n_blocks)
        def _():
            held[i] = kv_refs[i][...]

    def step(i, carry):
        work(i, blocks[0] + i, held.at[i])
        return carry

    lax.fori_loop(0, jnp.clip(n_blocks - blocks[0], 0, len(blocks)), step, 0)


def begin_kernel(len_ref, out_ref):
    tok = out_ref.shape[1]
    _, begin, _ = layout_of(len_ref, lax.axis_index(CTX), tok)
    out_ref[...] = begin


def d_attn_kernel(own_ref, pair_ref, cross_ref, diag_ref, w_ref, out_ref, rows):
    t = lax.axis_index("tensor")
    quarter = own_ref.shape[0]
    tok, hd = rows.shape[0], out_ref.shape[1]
    for mask, ref in enumerate((own_ref, pair_ref, cross_ref, diag_ref)):
        rows[pl.ds(pl.multiple_of((t ^ mask) * quarter, quarter), quarter), :] = ref[...]
    d_attn = dot_nt(rows[...], w_ref[...]).astype(BF16)
    for h in range(d_attn.shape[1] // hd):
        out_ref[h * tok : (h + 1) * tok, :] = d_attn[:, h * hd : (h + 1) * hd]


def forward_kernel(blocks, heads, scale, len_ref, begin_ref, q_ref, *refs):
    n = len(blocks)
    kv_refs = refs[:n]
    if blocks[0] == 0:
        top, denom, acc, held = refs[n:]
    else:
        top_in, denom_in, acc_in, attn_ref, lse_ref, held, top, denom, acc = refs[n:]
    tok, hd = q_ref.shape[0] // heads, q_ref.shape[1]
    me = lax.axis_index(CTX)
    q_pos, _, n_blocks = layout_of(len_ref, me, tok)
    begin = begin_ref[...]
    if blocks[0] == 0:
        top[...] = jnp.full(top.shape, NEG_FILL, F32)
        denom[...] = jnp.zeros(denom.shape, F32)
        acc[...] = jnp.zeros(acc.shape, F32)
    else:
        top[...] = top_in[...]
        denom[...] = denom_in[...]
        acc[...] = acc_in[...]

    def work(i, d, kv):
        v_t = kv[:, hd:].T
        bias = bias_of(q_pos, begin, (me - d) * tok, tok)
        s = dot_nt(kv[:, :hd], q_ref[...]) * (scale * LOG2E) + jnp.concatenate([bias] * heads, axis=1)
        old = top[...]
        new = jnp.maximum(old, jnp.max(s, axis=0, keepdims=True))
        p = jnp.exp2(s - new)
        shrink = jnp.exp2(old - new)
        top[...] = new
        denom[...] = denom[...] * shrink + jnp.sum(p, axis=0, keepdims=True)
        acc[...] = acc[...] * shrink + dot_nn(v_t, p.astype(BF16))

    each_block(blocks, kv_refs, held, n_blocks, work)
    if blocks[0] == 0:
        return
    lse_ref[...] = top[...] + jnp.log(denom[...]) * LOG2E
    for h in range(heads):
        cols = slice(h * tok, (h + 1) * tok)
        attn_ref[:, h * hd : (h + 1) * hd] = (acc[:, cols] / denom[:, cols]).T.astype(BF16)


def project_kernel(heads, attn_ref, g_ref, w_ref, send_ref, keep_ref, delta_ref, rows):
    t = lax.axis_index("tensor")
    tok = attn_ref.shape[0]
    hd = attn_ref.shape[1] // heads
    quarter, half = tok // 4, tok // 2
    for i, mask in enumerate((3, 1, 2, 0)):
        rows[i * quarter : (i + 1) * quarter, :] = attn_ref[pl.ds(pl.multiple_of((t ^ mask) * quarter, quarter), quarter), :]
    width = w_ref.shape[1]
    step = 512
    for n in range(width // step):
        cols = slice(n * step, (n + 1) * step)
        mixed = dot_nn(rows[...], w_ref[:, cols]).astype(BF16)
        send_ref[:, cols] = mixed[:half, :]
        keep_ref[:, cols] = mixed[half:, :]
    for h in range(heads):
        cols = slice(h * tok, (h + 1) * tok)
        prod = g_ref[cols, :].astype(F32) * attn_ref[:, h * hd : (h + 1) * hd].astype(F32)
        delta_ref[:, cols] = jnp.sum(prod.T, axis=0, keepdims=True)


def backward_kernel(blocks, first, last, heads, scale, len_ref, begin_ref, q_ref, *refs):
    n = len(blocks)
    kv_refs = refs[:n]
    g_ref, lse_ref, delta_ref = refs[n : n + 3]
    refs = refs[n + 3 :]
    if not first:
        dq_in, *refs = refs
    if last:
        dq_ref, *refs = refs
    else:
        dq_t, *refs = refs
    out_refs = refs[:n]
    held, terms = refs[n : n + 2]
    if last:
        dq_t = refs[n + 2]
    tok, hd = q_ref.shape[0] // heads, q_ref.shape[1]
    me = lax.axis_index(CTX)
    q_pos, _, n_blocks = layout_of(len_ref, me, tok)
    begin = begin_ref[...]
    dq_t[...] = jnp.zeros(dq_t.shape, F32) if first else dq_in[...]

    def work(i, d, kv):
        k = kv[:, :hd]
        bias = bias_of(q_pos, begin, (me - d) * tok, tok)
        s = dot_nt(k, q_ref[...]) * (scale * LOG2E) + jnp.concatenate([bias] * heads, axis=1)
        p = jnp.exp2(s - lse_ref[...])
        dp = dot_nt(kv[:, hd:], g_ref[...])
        ds = (p * (dp - delta_ref[...])).astype(BF16)
        out = out_refs[i] if n <= UNROLL else terms.at[i]
        out[:, :hd] = (dot_nn(ds, q_ref[...]) * scale).astype(BF16)
        out[:, hd:] = dot_nn(p.astype(BF16), g_ref[...]).astype(BF16)
        dq_t[...] = dq_t[...] + dot_nn(k.T, ds)

    each_block(blocks, kv_refs, held, n_blocks, work)
    for i, d in enumerate(blocks):
        if n > UNROLL:

            @pl.when(d < n_blocks)
            def _():
                out_refs[i][...] = terms[i]

        @pl.when(d >= n_blocks)
        def _():
            out_refs[i][...] = jnp.zeros(out_refs[i].shape, BF16)

    if last:
        for h in range(heads):
            dq_ref[:, h * hd : (h + 1) * hd] = (dq_t[:, h * tok : (h + 1) * tok] * scale).T.astype(BF16)


def finish_kernel(n_kv, *refs):
    sources = refs[:n_kv]
    dk_ref, dv_ref, held, sems = refs[n_kv:]
    copies = [pltpu.make_async_copy(ref, held.at[d], sems.at[d]) for d, ref in enumerate(sources)]
    for copy in copies:
        copy.start()
    for copy in copies:
        copy.wait()
    total = held[0].astype(F32)
    for d in range(1, n_kv):
        total = total + held[d].astype(F32)
    hd = dk_ref.shape[1]
    dk_ref[...] = total[:, :hd].astype(BF16)
    dv_ref[...] = total[:, hd:].astype(BF16)


def pair_sum_kernel(keep_ref, pair_ref, out_ref):
    n = out_ref.shape[0]
    out_ref[...] = (keep_ref[:n, :].astype(F32) + pair_ref[:n, :].astype(F32)).astype(BF16)


def mixed_sum_kernel(keep_ref, pair_ref, cross_ref, out_ref):
    n = out_ref.shape[0]
    total = keep_ref[n:, :].astype(F32) + pair_ref[n:, :].astype(F32) + cross_ref[...].astype(F32)
    out_ref[...] = total.astype(BF16)


def call(kernel, name, out_shape, args, scratch=(), smem=0, hbm=0, us=1.0, vmem_mb=24):
    vmem = pl.BlockSpec(memory_space=pltpu.VMEM)
    return pl.pallas_call(
        kernel,
        out_shape=out_shape,
        in_specs=[pl.BlockSpec(memory_space=pltpu.SMEM)] * smem
        + [pl.BlockSpec(memory_space=pltpu.HBM)] * hbm
        + [vmem] * (len(args) - smem - hbm),
        out_specs=jax.tree.map(lambda _: vmem, out_shape),
        scratch_shapes=list(scratch),
        compiler_params=pltpu.CompilerParams(vmem_limit_bytes=vmem_mb * 2**20),
        cost_estimate=pl.CostEstimate(flops=int(us * 1e9), bytes_accessed=0, transcendentals=0),
        name=name,
    )(*args)


def local(queries, keys, values, w_out, d_out, lengths):
    tok, heads, hd = queries.shape
    width = w_out.shape[2]
    ctx = lax.axis_size(CTX)
    longest = tok * ctx * 5 // 8
    reach = min(ctx - 1, -(-(longest - 1) // tok))
    n_kv = reach + 1
    split = min(n_kv, 4)
    scale = hd ** (-0.5)
    quarter = tok // 4
    n_tensor = lax.axis_size("tensor")
    shape = jax.ShapeDtypeStruct

    def swap(x, mask):
        return lax.ppermute(x, "tensor", [(i, i ^ mask) for i in range(n_tensor)])

    def shift(x, d):
        pairs = [(i, i + d) for i in range(ctx - d)] if d > 0 else [(i - d, i) for i in range(ctx + d)]
        return lax.ppermute(x, CTX, pairs)

    kv = jnp.concatenate([keys.reshape(tok, hd), values.reshape(tok, hd)], axis=1)
    w = w_out.reshape(heads * hd, width)
    pair = swap(d_out, 1)
    cross = swap(d_out, 2)
    kvs = [kv] + [shift(kv, d) for d in range(1, split)]
    kv_later, pair, queries, lengths, kvs[1] = lax.optimization_barrier((kv, pair, queries, lengths, kvs[1]))
    begin = call(begin_kernel, "begin", shape((1, tok), jnp.int32), (lengths,), smem=1, us=0.2)
    cross, begin = lax.optimization_barrier((cross, begin))
    q = queries.transpose(1, 0, 2).reshape(heads * tok, hd)
    kvs += [shift(kv_later, d) for d in range(split, n_kv)]
    near, far = list(range(split)), list(range(split, n_kv))
    row = shape((1, heads * tok), F32)
    state = (row, row, shape((hd, heads * tok), F32))
    held = pltpu.VMEM((split if split > UNROLL else 1, tok, 2 * hd), BF16)

    def blocks_of(group):
        return tuple(kvs[d] for d in group)

    begun = call(
        functools.partial(forward_kernel, near, heads, scale),
        "forward_near",
        state,
        (lengths, begin, q, *blocks_of(near)),
        scratch=(held,),
        smem=1,
        us=6.0,
    )
    begun, d_out = lax.optimization_barrier((begun, d_out))
    diag = swap(cross, 1)
    g = call(
        d_attn_kernel,
        "d_attn",
        shape((heads * tok, hd), BF16),
        (d_out, pair, cross, diag, w),
        scratch=(pltpu.VMEM((tok, width), BF16),),
        us=2.0,
    )
    begun, g = lax.optimization_barrier((begun, g))
    attn, lse = call(
        functools.partial(forward_kernel, far, heads, scale),
        "forward_far",
        (shape((tok, heads * hd), BF16), row),
        (lengths, begin, q, *blocks_of(far), *begun),
        scratch=(held,) + tuple(pltpu.VMEM(x.shape, F32) for x in state),
        smem=1,
        us=5.0,
    )
    send, keep, delta = call(
        functools.partial(project_kernel, heads),
        "project",
        (shape((tok // 2, width), BF16),) * 2 + (row,),
        (attn, g, w),
        scratch=(pltpu.VMEM((tok, heads * hd), BF16),),
        us=2.0,
    )
    from_pair = swap(send, 1)
    term = shape((tok, 2 * hd), BF16)

    def backward(blocks, name, us, dq=None, last=False):
        dq, *terms = call(
            functools.partial(backward_kernel, blocks, dq is None, last, heads, scale),
            name,
            (shape((tok, heads * hd), BF16) if last else state[2],) + (term,) * len(blocks),
            (lengths, begin, q, *blocks_of(blocks), g, lse, delta) + (() if dq is None else (dq,)),
            scratch=(held, held) + ((pltpu.VMEM(state[2].shape, F32),) if last else ()),
            smem=1,
            us=us,
        )
        return dq, dict(zip(blocks, terms))

    short = [1, lax.axis_size("inner")]
    if n_kv > UNROLL or short[1] not in range(2, n_kv):
        short = far
    dq, terms = backward([d for d in range(1, n_kv) if d not in short], "backward_first", 3.0)
    from_pair, dq = lax.optimization_barrier((from_pair, dq))
    back = {d: shift(terms[d], -d) for d in terms}
    early = max(back)
    to_cross = call(pair_sum_kernel, "pair_sum", shape((quarter, width), BF16), (keep, from_pair), us=0.5)
    from_cross = swap(to_cross, 2)
    dq, to_cross = lax.optimization_barrier((dq, to_cross))
    dq, terms = backward(short, "backward_second", 3.0, dq)
    terms[short[0]], back[early] = lax.optimization_barrier((terms[short[0]], back[early]))
    back.update({d: shift(terms[d], -d) for d in short})
    dq, terms = backward([0], "backward_own", 2.0, dq, True)
    back = [terms[0]] + [back[d] for d in range(1, n_kv)]
    mixed = call(mixed_sum_kernel, "mixed_sum", shape((quarter, width), BF16), (keep, from_pair, from_cross), us=0.5)
    back[0], mixed = lax.optimization_barrier((back[0], mixed))
    dk, dv = call(
        functools.partial(finish_kernel, n_kv),
        "finish",
        (shape((tok, hd), BF16),) * 2,
        tuple(back),
        scratch=(pltpu.VMEM((n_kv, tok, 2 * hd), BF16), pltpu.SemaphoreType.DMA((n_kv,))),
        hbm=n_kv,
        us=0.5,
        vmem_mb=60,
    )
    return (mixed, dq.reshape(tok, heads, hd), dk.reshape(tok, 1, hd), dv.reshape(tok, 1, hd))


def solution(mesh):
    return jax.shard_map(
        local,
        mesh=mesh,
        in_specs=(
            P(("outer", "inner"), "tensor", None),
            P(("outer", "inner"), "tensor", None),
            P(("outer", "inner"), "tensor", None),
            P("tensor", None, None),
            P(("outer", "inner", "tensor"), None),
            P(),
        ),
        out_specs=(
            P(("outer", "inner", "tensor"), None),
            P(("outer", "inner"), "tensor", None),
            P(("outer", "inner"), "tensor", None),
            P(("outer", "inner"), "tensor", None),
        ),
        check_vma=False,
    )
```

```python
import functools

import jax
import jax.numpy as jnp
from jax import lax
from jax.experimental import pallas as pl
from jax.experimental.pallas import tpu as pltpu
from jax.sharding import PartitionSpec as P

NEG_FILL = -1e30
LOG2E = 1.4426950408889634
CTX = ("outer", "inner")
F32 = jnp.float32
BF16 = jnp.bfloat16


def dot_nt(a, b):
    return lax.dot_general(a, b, (((1,), (1,)), ((), ())), preferred_element_type=F32)


def dot_nn(a, b):
    return jnp.dot(a, b, preferred_element_type=F32)


def places(begin_ref, me, tok):
    q_pos = me * tok + lax.broadcasted_iota(jnp.int32, (1, tok), 1)
    begin = begin_ref[...]
    return q_pos, begin, me - jnp.min(begin) // tok + 1


def bias_of(q_pos, begin, k_start, tok):
    k_pos = k_start + lax.broadcasted_iota(jnp.int32, (tok, tok), 0)
    return jnp.where((k_pos >= begin) & (k_pos <= q_pos), 0.0, NEG_FILL).astype(F32)


UNROLL = 8


def each_block(blocks, kv_refs, held, n_blocks, work):
    if len(blocks) <= UNROLL:
        for i, d in enumerate(blocks):

            @pl.when(d < n_blocks)
            def _():
                work(i, d, kv_refs[i])

        return
    for i, d in enumerate(blocks):

        @pl.when(d < n_blocks)
        def _():
            held[i] = kv_refs[i][...]

    def step(i, carry):
        work(i, blocks[0] + i, held.at[i])
        return carry

    lax.fori_loop(0, jnp.clip(n_blocks - blocks[0], 0, len(blocks)), step, 0)


def begin_kernel(len_ref, out_ref):
    tok = out_ref.shape[1]
    q_pos = lax.axis_index(CTX) * tok + lax.broadcasted_iota(jnp.int32, (1, tok), 1)
    begin = jnp.zeros((1, tok), jnp.int32)
    end = jnp.int32(0)
    for j in range(len_ref.shape[0]):
        end = end + len_ref[j]
        begin = jnp.where(q_pos >= end, end, begin)
    out_ref[...] = begin


def d_attn_kernel(own_ref, pair_ref, cross_ref, diag_ref, w_ref, out_ref, rows):
    t = lax.axis_index("tensor")
    quarter = own_ref.shape[0]
    tok, hd = rows.shape[0], out_ref.shape[1]
    for mask, ref in enumerate((own_ref, pair_ref, cross_ref, diag_ref)):
        rows[pl.ds(pl.multiple_of((t ^ mask) * quarter, quarter), quarter), :] = ref[...]
    d_attn = dot_nt(rows[...], w_ref[...]).astype(BF16)
    for h in range(d_attn.shape[1] // hd):
        out_ref[h * tok : (h + 1) * tok, :] = d_attn[:, h * hd : (h + 1) * hd]


def forward_kernel(blocks, heads, scale, begin_ref, q_ref, *refs):
    n = len(blocks)
    kv_refs = refs[:n]
    if blocks[0] == 0:
        top, denom, acc, held = refs[n:]
    else:
        top_in, denom_in, acc_in, attn_ref, lse_ref, held, top, denom, acc = refs[n:]
    tok, hd = q_ref.shape[0] // heads, q_ref.shape[1]
    me = lax.axis_index(CTX)
    q_pos, begin, n_blocks = places(begin_ref, me, tok)
    if blocks[0] == 0:
        top[...] = jnp.full(top.shape, NEG_FILL, F32)
        denom[...] = jnp.zeros(denom.shape, F32)
        acc[...] = jnp.zeros(acc.shape, F32)
    else:
        top[...] = top_in[...]
        denom[...] = denom_in[...]
        acc[...] = acc_in[...]

    def work(i, d, kv):
        v_t = kv[:, hd:].T
        bias = bias_of(q_pos, begin, (me - d) * tok, tok)
        s = dot_nt(kv[:, :hd], q_ref[...]) * (scale * LOG2E) + jnp.concatenate([bias] * heads, axis=1)
        old = top[...]
        new = jnp.maximum(old, jnp.max(s, axis=0, keepdims=True))
        p = jnp.exp2(s - new)
        shrink = jnp.exp2(old - new)
        top[...] = new
        denom[...] = denom[...] * shrink + jnp.sum(p, axis=0, keepdims=True)
        acc[...] = acc[...] * shrink + dot_nn(v_t, p.astype(BF16))

    each_block(blocks, kv_refs, held, n_blocks, work)
    if blocks[0] == 0:
        return
    lse_ref[...] = top[...] + jnp.log(denom[...]) * LOG2E
    for h in range(heads):
        cols = slice(h * tok, (h + 1) * tok)
        attn_ref[:, h * hd : (h + 1) * hd] = (acc[:, cols] / denom[:, cols]).T.astype(BF16)


def project_kernel(heads, attn_ref, g_ref, w_ref, send_ref, keep_ref, delta_ref, rows):
    t = lax.axis_index("tensor")
    tok = attn_ref.shape[0]
    hd = attn_ref.shape[1] // heads
    quarter, half = tok // 4, tok // 2
    for i, mask in enumerate((3, 1, 2, 0)):
        rows[i * quarter : (i + 1) * quarter, :] = attn_ref[pl.ds(pl.multiple_of((t ^ mask) * quarter, quarter), quarter), :]
    width = w_ref.shape[1]
    step = 512
    for n in range(width // step):
        cols = slice(n * step, (n + 1) * step)
        mixed = dot_nn(rows[...], w_ref[:, cols]).astype(BF16)
        send_ref[:, cols] = mixed[:half, :]
        keep_ref[:, cols] = mixed[half:, :]
    for h in range(heads):
        cols = slice(h * tok, (h + 1) * tok)
        prod = g_ref[cols, :].astype(F32) * attn_ref[:, h * hd : (h + 1) * hd].astype(F32)
        delta_ref[:, cols] = jnp.sum(prod.T, axis=0, keepdims=True)


def backward_kernel(blocks, first, last, heads, scale, begin_ref, q_ref, *refs):
    n = len(blocks)
    kv_refs = refs[:n]
    g_ref, lse_ref, delta_ref = refs[n : n + 3]
    refs = refs[n + 3 :]
    if not first:
        dq_in, *refs = refs
    if last:
        dq_ref, *refs = refs
    else:
        dq_t, *refs = refs
    out_refs = refs[:n]
    held, terms = refs[n : n + 2]
    if last:
        dq_t = refs[n + 2]
    tok, hd = q_ref.shape[0] // heads, q_ref.shape[1]
    me = lax.axis_index(CTX)
    q_pos, begin, n_blocks = places(begin_ref, me, tok)
    dq_t[...] = jnp.zeros(dq_t.shape, F32) if first else dq_in[...]

    def work(i, d, kv):
        k = kv[:, :hd]
        bias = bias_of(q_pos, begin, (me - d) * tok, tok)
        s = dot_nt(k, q_ref[...]) * (scale * LOG2E) + jnp.concatenate([bias] * heads, axis=1)
        p = jnp.exp2(s - lse_ref[...])
        dp = dot_nt(kv[:, hd:], g_ref[...])
        ds = (p * (dp - delta_ref[...])).astype(BF16)
        out = out_refs[i] if n <= UNROLL else terms.at[i]
        out[:, :hd] = (dot_nn(ds, q_ref[...]) * scale).astype(BF16)
        out[:, hd:] = dot_nn(p.astype(BF16), g_ref[...]).astype(BF16)
        dq_t[...] = dq_t[...] + dot_nn(k.T, ds)

    each_block(blocks, kv_refs, held, n_blocks, work)
    for i, d in enumerate(blocks):
        if n > UNROLL:

            @pl.when(d < n_blocks)
            def _():
                out_refs[i][...] = terms[i]

        @pl.when(d >= n_blocks)
        def _():
            out_refs[i][...] = jnp.zeros(out_refs[i].shape, BF16)

    if last:
        for h in range(heads):
            dq_ref[:, h * hd : (h + 1) * hd] = (dq_t[:, h * tok : (h + 1) * tok] * scale).T.astype(BF16)


def finish_kernel(n_kv, *refs):
    sources = refs[:n_kv]
    dk_ref, dv_ref, held, sems = refs[n_kv:]
    copies = [pltpu.make_async_copy(ref, held.at[d], sems.at[d]) for d, ref in enumerate(sources)]
    for copy in copies:
        copy.start()
    for copy in copies:
        copy.wait()
    total = held[0].astype(F32)
    for d in range(1, n_kv):
        total = total + held[d].astype(F32)
    hd = dk_ref.shape[1]
    dk_ref[...] = total[:, :hd].astype(BF16)
    dv_ref[...] = total[:, hd:].astype(BF16)


def pair_sum_kernel(keep_ref, pair_ref, out_ref):
    n = out_ref.shape[0]
    out_ref[...] = (keep_ref[:n, :].astype(F32) + pair_ref[:n, :].astype(F32)).astype(BF16)


def mixed_sum_kernel(keep_ref, pair_ref, cross_ref, out_ref):
    n = out_ref.shape[0]
    total = keep_ref[n:, :].astype(F32) + pair_ref[n:, :].astype(F32) + cross_ref[...].astype(F32)
    out_ref[...] = total.astype(BF16)


def call(kernel, name, out_shape, args, scratch=(), smem=0, hbm=0, us=1.0, vmem_mb=24):
    vmem = pl.BlockSpec(memory_space=pltpu.VMEM)
    return pl.pallas_call(
        kernel,
        out_shape=out_shape,
        in_specs=[pl.BlockSpec(memory_space=pltpu.SMEM)] * smem
        + [pl.BlockSpec(memory_space=pltpu.HBM)] * hbm
        + [vmem] * (len(args) - smem - hbm),
        out_specs=jax.tree.map(lambda _: vmem, out_shape),
        scratch_shapes=list(scratch),
        compiler_params=pltpu.CompilerParams(vmem_limit_bytes=vmem_mb * 2**20),
        cost_estimate=pl.CostEstimate(flops=int(us * 1e9), bytes_accessed=0, transcendentals=0),
        name=name,
    )(*args)


def local(queries, keys, values, w_out, d_out, lengths):
    tok, heads, hd = queries.shape
    width = w_out.shape[2]
    ctx = lax.axis_size(CTX)
    longest = tok * ctx * 5 // 8
    reach = min(ctx - 1, -(-(longest - 1) // tok))
    n_kv = reach + 1
    split = min(n_kv, 4)
    scale = hd ** (-0.5)
    quarter = tok // 4
    n_tensor = lax.axis_size("tensor")
    shape = jax.ShapeDtypeStruct

    def swap(x, mask):
        return lax.ppermute(x, "tensor", [(i, i ^ mask) for i in range(n_tensor)])

    def shift(x, d):
        pairs = [(i, i + d) for i in range(ctx - d)] if d > 0 else [(i - d, i) for i in range(ctx + d)]
        return lax.ppermute(x, CTX, pairs)

    kv = jnp.concatenate([keys.reshape(tok, hd), values.reshape(tok, hd)], axis=1)
    w = w_out.reshape(heads * hd, width)
    pair = swap(d_out, 1)
    cross = swap(d_out, 2)
    kvs = [kv] + [shift(kv, d) for d in range(1, split)]
    kv_later, pair, queries, lengths, kvs[1] = lax.optimization_barrier((kv, pair, queries, lengths, kvs[1]))
    begin = call(begin_kernel, "begin", shape((1, tok), jnp.int32), (lengths,), smem=1, us=0.2)
    cross, begin = lax.optimization_barrier((cross, begin))
    q = queries.transpose(1, 0, 2).reshape(heads * tok, hd)
    kvs += [shift(kv_later, d) for d in range(split, n_kv)]
    near, far = list(range(split)), list(range(split, n_kv))
    row = shape((1, heads * tok), F32)
    state = (row, row, shape((hd, heads * tok), F32))
    held = pltpu.VMEM((split if split > UNROLL else 1, tok, 2 * hd), BF16)

    def blocks_of(group):
        return tuple(kvs[d] for d in group)

    begun = call(
        functools.partial(forward_kernel, near, heads, scale),
        "forward_near",
        state,
        (begin, q, *blocks_of(near)),
        scratch=(held,),
        us=6.0,
    )
    begun, d_out = lax.optimization_barrier((begun, d_out))
    diag = swap(cross, 1)
    g = call(
        d_attn_kernel,
        "d_attn",
        shape((heads * tok, hd), BF16),
        (d_out, pair, cross, diag, w),
        scratch=(pltpu.VMEM((tok, width), BF16),),
        us=2.0,
    )
    begun, g = lax.optimization_barrier((begun, g))
    attn, lse = call(
        functools.partial(forward_kernel, far, heads, scale),
        "forward_far",
        (shape((tok, heads * hd), BF16), row),
        (begin, q, *blocks_of(far), *begun),
        scratch=(held,) + tuple(pltpu.VMEM(x.shape, F32) for x in state),
        us=5.0,
    )
    send, keep, delta = call(
        functools.partial(project_kernel, heads),
        "project",
        (shape((tok // 2, width), BF16),) * 2 + (row,),
        (attn, g, w),
        scratch=(pltpu.VMEM((tok, heads * hd), BF16),),
        us=2.0,
    )
    from_pair = swap(send, 1)
    term = shape((tok, 2 * hd), BF16)

    def backward(blocks, name, us, dq=None, last=False):
        dq, *terms = call(
            functools.partial(backward_kernel, blocks, dq is None, last, heads, scale),
            name,
            (shape((tok, heads * hd), BF16) if last else state[2],) + (term,) * len(blocks),
            (begin, q, *blocks_of(blocks), g, lse, delta) + (() if dq is None else (dq,)),
            scratch=(held, held) + ((pltpu.VMEM(state[2].shape, F32),) if last else ()),
            us=us,
        )
        return dq, dict(zip(blocks, terms))

    short = [1, lax.axis_size("inner")]
    if n_kv > UNROLL or short[1] not in range(2, n_kv):
        short = far
    dq, terms = backward([d for d in range(1, n_kv) if d not in short], "backward_first", 3.0)
    from_pair, dq = lax.optimization_barrier((from_pair, dq))
    back = {d: shift(terms[d], -d) for d in terms}
    early = max(back)
    to_cross = call(pair_sum_kernel, "pair_sum", shape((quarter, width), BF16), (keep, from_pair), us=0.5)
    from_cross = swap(to_cross, 2)
    dq, to_cross = lax.optimization_barrier((dq, to_cross))
    dq, terms = backward(short, "backward_second", 3.0, dq)
    terms[short[0]], back[early] = lax.optimization_barrier((terms[short[0]], back[early]))
    back.update({d: shift(terms[d], -d) for d in short})
    dq, terms = backward([0], "backward_own", 2.0, dq, True)
    back = [terms[0]] + [back[d] for d in range(1, n_kv)]
    mixed = call(mixed_sum_kernel, "mixed_sum", shape((quarter, width), BF16), (keep, from_pair, from_cross), us=0.5)
    back[0], mixed = lax.optimization_barrier((back[0], mixed))
    dk, dv = call(
        functools.partial(finish_kernel, n_kv),
        "finish",
        (shape((tok, hd), BF16),) * 2,
        tuple(back),
        scratch=(pltpu.VMEM((n_kv, tok, 2 * hd), BF16), pltpu.SemaphoreType.DMA((n_kv,))),
        hbm=n_kv,
        us=0.5,
        vmem_mb=60,
    )
    return (mixed, dq.reshape(tok, heads, hd), dk.reshape(tok, 1, hd), dv.reshape(tok, 1, hd))


def solution(mesh):
    return jax.shard_map(
        local,
        mesh=mesh,
        in_specs=(
            P(("outer", "inner"), "tensor", None),
            P(("outer", "inner"), "tensor", None),
            P(("outer", "inner"), "tensor", None),
            P("tensor", None, None),
            P(("outer", "inner", "tensor"), None),
            P(),
        ),
        out_specs=(
            P(("outer", "inner", "tensor"), None),
            P(("outer", "inner"), "tensor", None),
            P(("outer", "inner"), "tensor", None),
            P(("outer", "inner"), "tensor", None),
        ),
        check_vma=False,
    )
```

```python
import functools

import jax
import jax.numpy as jnp
from jax import lax
from jax.experimental import pallas as pl
from jax.experimental.pallas import tpu as pltpu
from jax.sharding import PartitionSpec as P

NEG_FILL = -1e30
LOG2E = 1.4426950408889634
CTX = ("outer", "inner")
F32 = jnp.float32
BF16 = jnp.bfloat16


def dot_nt(a, b):
    return lax.dot_general(a, b, (((1,), (1,)), ((), ())), preferred_element_type=F32)


def dot_nn(a, b):
    return jnp.dot(a, b, preferred_element_type=F32)


def places(begin_ref, me, tok):
    q_pos = me * tok + lax.broadcasted_iota(jnp.int32, (1, tok), 1)
    begin = begin_ref[...]
    return q_pos, begin, me - jnp.min(begin) // tok + 1


def bias_of(q_pos, begin, k_start, tok):
    k_pos = k_start + lax.broadcasted_iota(jnp.int32, (tok, tok), 0)
    return jnp.where((k_pos >= begin) & (k_pos <= q_pos), 0.0, NEG_FILL).astype(F32)


UNROLL = 8


def each_block(blocks, kv_refs, held, n_blocks, work):
    if len(blocks) <= UNROLL:
        for i, d in enumerate(blocks):

            @pl.when(d < n_blocks)
            def _():
                work(i, d, kv_refs[i])

        return
    for i, d in enumerate(blocks):

        @pl.when(d < n_blocks)
        def _():
            held[i] = kv_refs[i][...]

    def step(i, carry):
        work(i, blocks[0] + i, held.at[i])
        return carry

    lax.fori_loop(0, jnp.clip(n_blocks - blocks[0], 0, len(blocks)), step, 0)


def begin_kernel(len_ref, out_ref):
    tok = out_ref.shape[1]
    q_pos = lax.axis_index(CTX) * tok + lax.broadcasted_iota(jnp.int32, (1, tok), 1)
    begin = jnp.zeros((1, tok), jnp.int32)
    end = jnp.int32(0)
    for j in range(len_ref.shape[0]):
        end = end + len_ref[j]
        begin = jnp.where(q_pos >= end, end, begin)
    out_ref[...] = begin


def d_attn_kernel(own_ref, pair_ref, cross_ref, diag_ref, w_ref, out_ref, rows):
    t = lax.axis_index("tensor")
    quarter = own_ref.shape[0]
    tok, hd = rows.shape[0], out_ref.shape[1]
    for mask, ref in enumerate((own_ref, pair_ref, cross_ref, diag_ref)):
        rows[pl.ds(pl.multiple_of((t ^ mask) * quarter, quarter), quarter), :] = ref[...]
    d_attn = dot_nt(rows[...], w_ref[...]).astype(BF16)
    for h in range(d_attn.shape[1] // hd):
        out_ref[h * tok : (h + 1) * tok, :] = d_attn[:, h * hd : (h + 1) * hd]


def forward_kernel(blocks, heads, scale, begin_ref, q_ref, *refs):
    n = len(blocks)
    kv_refs = refs[:n]
    if blocks[0] == 0:
        top, denom, acc, held = refs[n:]
    else:
        top_in, denom_in, acc_in, attn_ref, lse_ref, held, top, denom, acc = refs[n:]
    tok, hd = q_ref.shape[0] // heads, q_ref.shape[1]
    me = lax.axis_index(CTX)
    q_pos, begin, n_blocks = places(begin_ref, me, tok)
    if blocks[0] == 0:
        top[...] = jnp.full(top.shape, NEG_FILL, F32)
        denom[...] = jnp.zeros(denom.shape, F32)
        acc[...] = jnp.zeros(acc.shape, F32)
    else:
        top[...] = top_in[...]
        denom[...] = denom_in[...]
        acc[...] = acc_in[...]

    def work(i, d, kv):
        v_t = kv[:, hd:].T
        bias = bias_of(q_pos, begin, (me - d) * tok, tok)
        s = dot_nt(kv[:, :hd], q_ref[...]) * (scale * LOG2E) + jnp.concatenate([bias] * heads, axis=1)
        old = top[...]
        new = jnp.maximum(old, jnp.max(s, axis=0, keepdims=True))
        p = jnp.exp2(s - new)
        shrink = jnp.exp2(old - new)
        top[...] = new
        denom[...] = denom[...] * shrink + jnp.sum(p, axis=0, keepdims=True)
        acc[...] = acc[...] * shrink + dot_nn(v_t, p.astype(BF16))

    each_block(blocks, kv_refs, held, n_blocks, work)
    if blocks[0] == 0:
        return
    lse_ref[...] = top[...] + jnp.log(denom[...]) * LOG2E
    for h in range(heads):
        cols = slice(h * tok, (h + 1) * tok)
        attn_ref[:, h * hd : (h + 1) * hd] = (acc[:, cols] / denom[:, cols]).T.astype(BF16)


def project_kernel(heads, attn_ref, g_ref, w_ref, send_ref, keep_ref, delta_ref, rows):
    t = lax.axis_index("tensor")
    tok = attn_ref.shape[0]
    hd = attn_ref.shape[1] // heads
    quarter, half = tok // 4, tok // 2
    for i, mask in enumerate((3, 1, 2, 0)):
        rows[i * quarter : (i + 1) * quarter, :] = attn_ref[pl.ds(pl.multiple_of((t ^ mask) * quarter, quarter), quarter), :]
    width = w_ref.shape[1]
    step = 512
    for n in range(width // step):
        cols = slice(n * step, (n + 1) * step)
        mixed = dot_nn(rows[...], w_ref[:, cols]).astype(BF16)
        send_ref[:, cols] = mixed[:half, :]
        keep_ref[:, cols] = mixed[half:, :]
    for h in range(heads):
        cols = slice(h * tok, (h + 1) * tok)
        prod = g_ref[cols, :].astype(F32) * attn_ref[:, h * hd : (h + 1) * hd].astype(F32)
        delta_ref[:, cols] = jnp.sum(prod.T, axis=0, keepdims=True)


def backward_kernel(blocks, first, last, heads, scale, begin_ref, q_ref, *refs):
    n = len(blocks)
    kv_refs = refs[:n]
    g_ref, lse_ref, delta_ref = refs[n : n + 3]
    refs = refs[n + 3 :]
    if not first:
        dq_in, *refs = refs
    if last:
        dq_ref, *refs = refs
    else:
        dq_t, *refs = refs
    out_refs = refs[:n]
    held, terms = refs[n : n + 2]
    if last:
        dq_t = refs[n + 2]
    tok, hd = q_ref.shape[0] // heads, q_ref.shape[1]
    me = lax.axis_index(CTX)
    q_pos, begin, n_blocks = places(begin_ref, me, tok)
    dq_t[...] = jnp.zeros(dq_t.shape, F32) if first else dq_in[...]

    def work(i, d, kv):
        k = kv[:, :hd]
        bias = bias_of(q_pos, begin, (me - d) * tok, tok)
        s = dot_nt(k, q_ref[...]) * (scale * LOG2E) + jnp.concatenate([bias] * heads, axis=1)
        p = jnp.exp2(s - lse_ref[...])
        dp = dot_nt(kv[:, hd:], g_ref[...])
        ds = (p * (dp - delta_ref[...])).astype(BF16)
        out = out_refs[i] if n <= UNROLL else terms.at[i]
        out[:, :hd] = (dot_nn(ds, q_ref[...]) * scale).astype(BF16)
        out[:, hd:] = dot_nn(p.astype(BF16), g_ref[...]).astype(BF16)
        dq_t[...] = dq_t[...] + dot_nn(k.T, ds)

    each_block(blocks, kv_refs, held, n_blocks, work)
    for i, d in enumerate(blocks):
        if n > UNROLL:

            @pl.when(d < n_blocks)
            def _():
                out_refs[i][...] = terms[i]

        @pl.when(d >= n_blocks)
        def _():
            out_refs[i][...] = jnp.zeros(out_refs[i].shape, BF16)

    if last:
        for h in range(heads):
            dq_ref[:, h * hd : (h + 1) * hd] = (dq_t[:, h * tok : (h + 1) * tok] * scale).T.astype(BF16)


def finish_kernel(n_kv, *refs):
    sources = refs[:n_kv]
    outs, held, sums, sems, out_sems = refs[n_kv : n_kv + 2], *refs[n_kv + 2 :]
    parts, hd = out_sems.shape[0], outs[0].shape[1]
    step = outs[0].shape[0] // parts
    rows = [slice(j * step, (j + 1) * step) for j in range(parts)]
    copies = [
        [pltpu.make_async_copy(ref.at[r, :], held.at[d, r, :], sems.at[j, d]) for d, ref in enumerate(sources)]
        for j, r in enumerate(rows)
    ]
    for part in copies:
        for copy in part:
            copy.start()
    sends = []
    for j, r in enumerate(rows):
        for copy in copies[j]:
            copy.wait()
        total = held[0, r, :].astype(F32)
        for d in range(1, n_kv):
            total = total + held[d, r, :].astype(F32)
        for i, out in enumerate(outs):
            sums[i, r, :] = total[:, i * hd : (i + 1) * hd].astype(BF16)
            sends.append(pltpu.make_async_copy(sums.at[i, r, :], out.at[r, :], out_sems.at[j, i]))
            sends[-1].start()
    for copy in sends:
        copy.wait()


def pair_sum_kernel(keep_ref, pair_ref, out_ref):
    n = out_ref.shape[0]
    out_ref[...] = (keep_ref[:n, :].astype(F32) + pair_ref[:n, :].astype(F32)).astype(BF16)


def mixed_sum_kernel(keep_ref, pair_ref, cross_ref, out_ref):
    n = out_ref.shape[0]
    total = keep_ref[n:, :].astype(F32) + pair_ref[n:, :].astype(F32) + cross_ref[...].astype(F32)
    out_ref[...] = total.astype(BF16)


def call(kernel, name, out_shape, args, scratch=(), smem=0, hbm=0, out_hbm=False, us=1.0, vmem_mb=24):
    vmem = pl.BlockSpec(memory_space=pltpu.VMEM)
    return pl.pallas_call(
        kernel,
        out_shape=out_shape,
        in_specs=[pl.BlockSpec(memory_space=pltpu.SMEM)] * smem
        + [pl.BlockSpec(memory_space=pltpu.HBM)] * hbm
        + [vmem] * (len(args) - smem - hbm),
        out_specs=jax.tree.map(lambda _: pl.BlockSpec(memory_space=pl.ANY) if out_hbm else vmem, out_shape),
        scratch_shapes=list(scratch),
        compiler_params=pltpu.CompilerParams(vmem_limit_bytes=vmem_mb * 2**20),
        cost_estimate=pl.CostEstimate(flops=int(us * 1e9), bytes_accessed=0, transcendentals=0),
        name=name,
    )(*args)


def local(queries, keys, values, w_out, d_out, lengths):
    tok, heads, hd = queries.shape
    width = w_out.shape[2]
    ctx = lax.axis_size(CTX)
    longest = tok * ctx * 5 // 8
    reach = min(ctx - 1, -(-(longest - 1) // tok))
    n_kv = reach + 1
    split = min(n_kv, 4)
    scale = hd ** (-0.5)
    quarter = tok // 4
    n_tensor = lax.axis_size("tensor")
    shape = jax.ShapeDtypeStruct

    def swap(x, mask):
        return lax.ppermute(x, "tensor", [(i, i ^ mask) for i in range(n_tensor)])

    def shift(x, d):
        pairs = [(i, i + d) for i in range(ctx - d)] if d > 0 else [(i - d, i) for i in range(ctx + d)]
        return lax.ppermute(x, CTX, pairs)

    kv = jnp.concatenate([keys.reshape(tok, hd), values.reshape(tok, hd)], axis=1)
    w = w_out.reshape(heads * hd, width)
    pair = swap(d_out, 1)
    cross = swap(d_out, 2)
    kvs = [kv] + [shift(kv, d) for d in range(1, split)]
    kv_later, pair, queries, lengths, kvs[1] = lax.optimization_barrier((kv, pair, queries, lengths, kvs[1]))
    begin = call(begin_kernel, "begin", shape((1, tok), jnp.int32), (lengths,), smem=1, us=0.2)
    cross, begin = lax.optimization_barrier((cross, begin))
    q = queries.transpose(1, 0, 2).reshape(heads * tok, hd)
    kvs += [shift(kv_later, d) for d in range(split, n_kv)]
    near, far = list(range(split)), list(range(split, n_kv))
    row = shape((1, heads * tok), F32)
    state = (row, row, shape((hd, heads * tok), F32))
    held = pltpu.VMEM((split if split > UNROLL else 1, tok, 2 * hd), BF16)

    def blocks_of(group):
        return tuple(kvs[d] for d in group)

    begun = call(
        functools.partial(forward_kernel, near, heads, scale),
        "forward_near",
        state,
        (begin, q, *blocks_of(near)),
        scratch=(held,),
        us=6.0,
    )
    begun, d_out = lax.optimization_barrier((begun, d_out))
    diag = swap(cross, 1)
    g = call(
        d_attn_kernel,
        "d_attn",
        shape((heads * tok, hd), BF16),
        (d_out, pair, cross, diag, w),
        scratch=(pltpu.VMEM((tok, width), BF16),),
        us=2.0,
    )
    begun, g = lax.optimization_barrier((begun, g))
    attn, lse = call(
        functools.partial(forward_kernel, far, heads, scale),
        "forward_far",
        (shape((tok, heads * hd), BF16), row),
        (begin, q, *blocks_of(far), *begun),
        scratch=(held,) + tuple(pltpu.VMEM(x.shape, F32) for x in state),
        us=5.0,
    )
    send, keep, delta = call(
        functools.partial(project_kernel, heads),
        "project",
        (shape((tok // 2, width), BF16),) * 2 + (row,),
        (attn, g, w),
        scratch=(pltpu.VMEM((tok, heads * hd), BF16),),
        us=2.0,
    )
    from_pair = swap(send, 1)
    term = shape((tok, 2 * hd), BF16)

    def backward(blocks, name, us, dq=None, last=False):
        dq, *terms = call(
            functools.partial(backward_kernel, blocks, dq is None, last, heads, scale),
            name,
            (shape((tok, heads * hd), BF16) if last else state[2],) + (term,) * len(blocks),
            (begin, q, *blocks_of(blocks), g, lse, delta) + (() if dq is None else (dq,)),
            scratch=(held, held) + ((pltpu.VMEM(state[2].shape, F32),) if last else ()),
            us=us,
        )
        return dq, dict(zip(blocks, terms))

    short = [1, lax.axis_size("inner")]
    if n_kv > UNROLL or short[1] not in range(2, n_kv):
        short = far
    dq, terms = backward([d for d in range(1, n_kv) if d not in short], "backward_first", 3.0)
    from_pair, dq = lax.optimization_barrier((from_pair, dq))
    back = {d: shift(terms[d], -d) for d in terms}
    early = max(back)
    to_cross = call(pair_sum_kernel, "pair_sum", shape((quarter, width), BF16), (keep, from_pair), us=0.5)
    from_cross = swap(to_cross, 2)
    dq, to_cross = lax.optimization_barrier((dq, to_cross))
    dq, terms = backward(short, "backward_second", 3.0, dq)
    terms[short[0]], back[early] = lax.optimization_barrier((terms[short[0]], back[early]))
    back.update({d: shift(terms[d], -d) for d in short})
    dq, terms = backward([0], "backward_own", 2.0, dq, True)
    back = [terms[0]] + [back[d] for d in range(1, n_kv)]
    mixed = call(mixed_sum_kernel, "mixed_sum", shape((quarter, width), BF16), (keep, from_pair, from_cross), us=0.5)
    back[0], mixed = lax.optimization_barrier((back[0], mixed))
    dk, dv = call(
        functools.partial(finish_kernel, n_kv),
        "finish",
        (shape((tok, hd), BF16),) * 2,
        tuple(back),
        scratch=(
            pltpu.VMEM((n_kv, tok, 2 * hd), BF16),
            pltpu.VMEM((2, tok, hd), BF16),
            pltpu.SemaphoreType.DMA((2, n_kv)),
            pltpu.SemaphoreType.DMA((2, 2)),
        ),
        hbm=n_kv,
        out_hbm=True,
        us=0.5,
        vmem_mb=60,
    )
    return (mixed, dq.reshape(tok, heads, hd), dk.reshape(tok, 1, hd), dv.reshape(tok, 1, hd))


def solution(mesh):
    return jax.shard_map(
        local,
        mesh=mesh,
        in_specs=(
            P(("outer", "inner"), "tensor", None),
            P(("outer", "inner"), "tensor", None),
            P(("outer", "inner"), "tensor", None),
            P("tensor", None, None),
            P(("outer", "inner", "tensor"), None),
            P(),
        ),
        out_specs=(
            P(("outer", "inner", "tensor"), None),
            P(("outer", "inner"), "tensor", None),
            P(("outer", "inner"), "tensor", None),
            P(("outer", "inner"), "tensor", None),
        ),
        check_vma=False,
    )
```

```python
import functools

import jax
import jax.numpy as jnp
from jax import lax
from jax.experimental import pallas as pl
from jax.experimental.pallas import tpu as pltpu
from jax.sharding import PartitionSpec as P

NEG_FILL = -1e30
LOG2E = 1.4426950408889634
CTX = ("outer", "inner")
F32 = jnp.float32
BF16 = jnp.bfloat16


def dot_nt(a, b):
    return lax.dot_general(a, b, (((1,), (1,)), ((), ())), preferred_element_type=F32)


def dot_nn(a, b):
    return jnp.dot(a, b, preferred_element_type=F32)


def places(begin_ref, me, tok):
    q_pos = me * tok + lax.broadcasted_iota(jnp.int32, (1, tok), 1)
    begin = begin_ref[...]
    return q_pos, begin, me - jnp.min(begin) // tok + 1


def bias_of(q_pos, begin, k_start, tok):
    k_pos = k_start + lax.broadcasted_iota(jnp.int32, (tok, tok), 0)
    return jnp.where((k_pos >= begin) & (k_pos <= q_pos), 0.0, NEG_FILL).astype(F32)


UNROLL = 8


def each_block(blocks, kv_refs, held, n_blocks, work):
    if len(blocks) <= UNROLL:
        for i, d in enumerate(blocks):

            @pl.when(d < n_blocks)
            def _():
                work(i, d, kv_refs[i])

        return
    for i, d in enumerate(blocks):

        @pl.when(d < n_blocks)
        def _():
            held[i] = kv_refs[i][...]

    def step(i, carry):
        work(i, blocks[0] + i, held.at[i])
        return carry

    lax.fori_loop(0, jnp.clip(n_blocks - blocks[0], 0, len(blocks)), step, 0)


def begin_kernel(len_ref, out_ref):
    tok = out_ref.shape[1]
    q_pos = lax.axis_index(CTX) * tok + lax.broadcasted_iota(jnp.int32, (1, tok), 1)
    begin = jnp.zeros((1, tok), jnp.int32)
    end = jnp.int32(0)
    for j in range(len_ref.shape[0]):
        end = end + len_ref[j]
        begin = jnp.where(q_pos >= end, end, begin)
    out_ref[...] = begin


def d_attn_kernel(own_ref, pair_ref, cross_ref, diag_ref, w_ref, out_ref, rows):
    t = lax.axis_index("tensor")
    quarter = own_ref.shape[0]
    tok, hd = rows.shape[0], out_ref.shape[1]
    for mask, ref in enumerate((own_ref, pair_ref, cross_ref, diag_ref)):
        rows[pl.ds(pl.multiple_of((t ^ mask) * quarter, quarter), quarter), :] = ref[...]
    d_attn = dot_nt(rows[...], w_ref[...]).astype(BF16)
    for h in range(d_attn.shape[1] // hd):
        out_ref[h * tok : (h + 1) * tok, :] = d_attn[:, h * hd : (h + 1) * hd]


def forward_kernel(blocks, heads, scale, begin_ref, q_ref, *refs):
    n = len(blocks)
    kv_refs = refs[:n]
    if blocks[0] == 0:
        top, denom, acc, held = refs[n:]
    else:
        top_in, denom_in, acc_in, attn_ref, lse_ref, held, top, denom, acc = refs[n:]
    tok, hd = q_ref.shape[0] // heads, q_ref.shape[1]
    me = lax.axis_index(CTX)
    q_pos, begin, n_blocks = places(begin_ref, me, tok)
    if blocks[0] == 0:
        top[...] = jnp.full(top.shape, NEG_FILL, F32)
        denom[...] = jnp.zeros(denom.shape, F32)
        acc[...] = jnp.zeros(acc.shape, F32)
    else:
        top[...] = top_in[...]
        denom[...] = denom_in[...]
        acc[...] = acc_in[...]

    def work(i, d, kv):
        v_t = kv[:, hd:].T
        bias = bias_of(q_pos, begin, (me - d) * tok, tok)
        s = dot_nt(kv[:, :hd], q_ref[...]) * (scale * LOG2E) + jnp.concatenate([bias] * heads, axis=1)
        old = top[...]
        new = jnp.maximum(old, jnp.max(s, axis=0, keepdims=True))
        p = jnp.exp2(s - new)
        shrink = jnp.exp2(old - new)
        top[...] = new
        denom[...] = denom[...] * shrink + jnp.sum(p, axis=0, keepdims=True)
        acc[...] = acc[...] * shrink + dot_nn(v_t, p.astype(BF16))

    each_block(blocks, kv_refs, held, n_blocks, work)
    if blocks[0] == 0:
        return
    lse_ref[...] = top[...] + jnp.log(denom[...]) * LOG2E
    for h in range(heads):
        cols = slice(h * tok, (h + 1) * tok)
        attn_ref[:, h * hd : (h + 1) * hd] = (acc[:, cols] / denom[:, cols]).T.astype(BF16)


def project_kernel(heads, attn_ref, g_ref, w_ref, send_ref, keep_ref, delta_ref, rows):
    t = lax.axis_index("tensor")
    tok = attn_ref.shape[0]
    hd = attn_ref.shape[1] // heads
    quarter, half = tok // 4, tok // 2
    for i, mask in enumerate((3, 1, 2, 0)):
        rows[i * quarter : (i + 1) * quarter, :] = attn_ref[pl.ds(pl.multiple_of((t ^ mask) * quarter, quarter), quarter), :]
    width = w_ref.shape[1]
    step = 512
    for n in range(width // step):
        cols = slice(n * step, (n + 1) * step)
        mixed = dot_nn(rows[...], w_ref[:, cols]).astype(BF16)
        send_ref[:, cols] = mixed[:half, :]
        keep_ref[:, cols] = mixed[half:, :]
    for h in range(heads):
        cols = slice(h * tok, (h + 1) * tok)
        prod = g_ref[cols, :].astype(F32) * attn_ref[:, h * hd : (h + 1) * hd].astype(F32)
        delta_ref[:, cols] = jnp.sum(prod.T, axis=0, keepdims=True)


def backward_kernel(blocks, first, last, heads, scale, begin_ref, q_ref, *refs):
    n = len(blocks)
    kv_refs = refs[:n]
    g_ref, lse_ref, delta_ref = refs[n : n + 3]
    refs = refs[n + 3 :]
    if not first:
        dq_in, *refs = refs
    if last:
        dq_ref, *refs = refs
    else:
        dq_t, *refs = refs
    out_refs = refs[:n]
    held, terms = refs[n : n + 2]
    if last:
        dq_t = refs[n + 2]
    tok, hd = q_ref.shape[0] // heads, q_ref.shape[1]
    me = lax.axis_index(CTX)
    q_pos, begin, n_blocks = places(begin_ref, me, tok)
    dq_t[...] = jnp.zeros(dq_t.shape, F32) if first else dq_in[...]

    def work(i, d, kv):
        k = kv[:, :hd]
        bias = bias_of(q_pos, begin, (me - d) * tok, tok)
        s = dot_nt(k, q_ref[...]) * (scale * LOG2E) + jnp.concatenate([bias] * heads, axis=1)
        p = jnp.exp2(s - lse_ref[...])
        dp = dot_nt(kv[:, hd:], g_ref[...])
        ds = (p * (dp - delta_ref[...])).astype(BF16)
        out = out_refs[i] if n <= UNROLL else terms.at[i]
        out[:, :hd] = (dot_nn(ds, q_ref[...]) * scale).astype(BF16)
        out[:, hd:] = dot_nn(p.astype(BF16), g_ref[...]).astype(BF16)
        dq_t[...] = dq_t[...] + dot_nn(k.T, ds)

    each_block(blocks, kv_refs, held, n_blocks, work)
    for i, d in enumerate(blocks):
        if n > UNROLL:

            @pl.when(d < n_blocks)
            def _():
                out_refs[i][...] = terms[i]

        @pl.when(d >= n_blocks)
        def _():
            out_refs[i][...] = jnp.zeros(out_refs[i].shape, BF16)

    if last:
        for h in range(heads):
            dq_ref[:, h * hd : (h + 1) * hd] = (dq_t[:, h * tok : (h + 1) * tok] * scale).T.astype(BF16)


def finish_kernel(n_kv, *refs):
    sources = refs[:n_kv]
    dk_ref, dv_ref, held, sems = refs[n_kv:]
    copies = [pltpu.make_async_copy(ref, held.at[d], sems.at[d]) for d, ref in enumerate(sources)]
    for copy in copies:
        copy.start()
    for copy in copies:
        copy.wait()
    total = held[0].astype(F32)
    for d in range(1, n_kv):
        total = total + held[d].astype(F32)
    hd = dk_ref.shape[1]
    dk_ref[...] = total[:, :hd].astype(BF16)
    dv_ref[...] = total[:, hd:].astype(BF16)


def pair_sum_kernel(keep_ref, pair_ref, out_ref):
    n = out_ref.shape[0]
    out_ref[...] = (keep_ref[:n, :].astype(F32) + pair_ref[:n, :].astype(F32)).astype(BF16)


def mixed_sum_kernel(keep_ref, pair_ref, cross_ref, out_ref):
    n = out_ref.shape[0]
    total = keep_ref[n:, :].astype(F32) + pair_ref[n:, :].astype(F32) + cross_ref[...].astype(F32)
    out_ref[...] = total.astype(BF16)


def call(kernel, name, out_shape, args, scratch=(), smem=0, hbm=0, us=1.0, vmem_mb=24):
    vmem = pl.BlockSpec(memory_space=pltpu.VMEM)
    return pl.pallas_call(
        kernel,
        out_shape=out_shape,
        in_specs=[pl.BlockSpec(memory_space=pltpu.SMEM)] * smem
        + [pl.BlockSpec(memory_space=pltpu.HBM)] * hbm
        + [vmem] * (len(args) - smem - hbm),
        out_specs=jax.tree.map(lambda _: vmem, out_shape),
        scratch_shapes=list(scratch),
        compiler_params=pltpu.CompilerParams(vmem_limit_bytes=vmem_mb * 2**20),
        cost_estimate=pl.CostEstimate(flops=int(us * 1e9), bytes_accessed=0, transcendentals=0),
        name=name,
    )(*args)


def local(queries, keys, values, w_out, d_out, lengths):
    tok, heads, hd = queries.shape
    width = w_out.shape[2]
    ctx = lax.axis_size(CTX)
    longest = tok * ctx * 5 // 8
    reach = min(ctx - 1, -(-(longest - 1) // tok))
    n_kv = reach + 1
    split = min(n_kv, 4)
    scale = hd ** (-0.5)
    quarter = tok // 4
    n_tensor = lax.axis_size("tensor")
    shape = jax.ShapeDtypeStruct

    def swap(x, mask):
        return lax.ppermute(x, "tensor", [(i, i ^ mask) for i in range(n_tensor)])

    def shift(x, d):
        pairs = [(i, i + d) for i in range(ctx - d)] if d > 0 else [(i - d, i) for i in range(ctx + d)]
        return lax.ppermute(x, CTX, pairs)

    kv = jnp.concatenate([keys.reshape(tok, hd), values.reshape(tok, hd)], axis=1)
    w = w_out.reshape(heads * hd, width)
    pair = swap(d_out, 1)
    cross = swap(d_out, 2)
    kvs = [kv] + [shift(kv, d) for d in range(1, split)]
    kv_later, pair, queries, lengths, kvs[1] = lax.optimization_barrier((kv, pair, queries, lengths, kvs[1]))
    begin = call(begin_kernel, "begin", shape((1, tok), jnp.int32), (lengths,), smem=1, us=0.2)
    cross, begin = lax.optimization_barrier((cross, begin))
    q = queries.transpose(1, 0, 2).reshape(heads * tok, hd)
    kvs += [shift(kv_later, d) for d in range(split, n_kv)]
    near, far = list(range(split)), list(range(split, n_kv))
    row = shape((1, heads * tok), F32)
    state = (row, row, shape((hd, heads * tok), F32))
    held = pltpu.VMEM((split if split > UNROLL else 1, tok, 2 * hd), BF16)

    def blocks_of(group):
        return tuple(kvs[d] for d in group)

    begun = call(
        functools.partial(forward_kernel, near, heads, scale),
        "forward_near",
        state,
        (begin, q, *blocks_of(near)),
        scratch=(held,),
        us=6.0,
    )
    begun, d_out = lax.optimization_barrier((begun, d_out))
    diag = swap(cross, 1)
    g = call(
        d_attn_kernel,
        "d_attn",
        shape((heads * tok, hd), BF16),
        (d_out, pair, cross, diag, w),
        scratch=(pltpu.VMEM((tok, width), BF16),),
        us=2.0,
    )
    begun, g = lax.optimization_barrier((begun, g))
    attn, lse = call(
        functools.partial(forward_kernel, far, heads, scale),
        "forward_far",
        (shape((tok, heads * hd), BF16), row),
        (begin, q, *blocks_of(far), *begun),
        scratch=(held,) + tuple(pltpu.VMEM(x.shape, F32) for x in state),
        us=5.0,
    )
    send, keep, delta = call(
        functools.partial(project_kernel, heads),
        "project",
        (shape((tok // 2, width), BF16),) * 2 + (row,),
        (attn, g, w),
        scratch=(pltpu.VMEM((tok, heads * hd), BF16),),
        us=2.0,
    )
    from_pair = swap(send, 1)
    term = shape((tok, 2 * hd), BF16)

    def backward(blocks, name, us, dq=None, last=False):
        dq, *terms = call(
            functools.partial(backward_kernel, blocks, dq is None, last, heads, scale),
            name,
            (shape((tok, heads * hd), BF16) if last else state[2],) + (term,) * len(blocks),
            (begin, q, *blocks_of(blocks), g, lse, delta) + (() if dq is None else (dq,)),
            scratch=(held, held) + ((pltpu.VMEM(state[2].shape, F32),) if last else ()),
            us=us,
        )
        return dq, dict(zip(blocks, terms))

    short = [1] if n_kv <= UNROLL else far
    dq, terms = backward([d for d in range(1, n_kv) if d not in short], "backward_first", 3.0)
    from_pair, dq = lax.optimization_barrier((from_pair, dq))
    back = {d: shift(terms[d], -d) for d in terms}
    early = max(back)
    to_cross = call(pair_sum_kernel, "pair_sum", shape((quarter, width), BF16), (keep, from_pair), us=0.5)
    from_cross = swap(to_cross, 2)
    dq, to_cross = lax.optimization_barrier((dq, to_cross))
    dq, terms = backward(short, "backward_second", 3.0, dq)
    terms[short[0]], back[early] = lax.optimization_barrier((terms[short[0]], back[early]))
    back.update({d: shift(terms[d], -d) for d in short})
    dq, terms = backward([0], "backward_own", 2.0, dq, True)
    back = [terms[0]] + [back[d] for d in range(1, n_kv)]
    mixed = call(mixed_sum_kernel, "mixed_sum", shape((quarter, width), BF16), (keep, from_pair, from_cross), us=0.5)
    back[0], mixed = lax.optimization_barrier((back[0], mixed))
    dk, dv = call(
        functools.partial(finish_kernel, n_kv),
        "finish",
        (shape((tok, hd), BF16),) * 2,
        tuple(back),
        scratch=(pltpu.VMEM((n_kv, tok, 2 * hd), BF16), pltpu.SemaphoreType.DMA((n_kv,))),
        hbm=n_kv,
        us=0.5,
        vmem_mb=60,
    )
    return (mixed, dq.reshape(tok, heads, hd), dk.reshape(tok, 1, hd), dv.reshape(tok, 1, hd))


def solution(mesh):
    return jax.shard_map(
        local,
        mesh=mesh,
        in_specs=(
            P(("outer", "inner"), "tensor", None),
            P(("outer", "inner"), "tensor", None),
            P(("outer", "inner"), "tensor", None),
            P("tensor", None, None),
            P(("outer", "inner", "tensor"), None),
            P(),
        ),
        out_specs=(
            P(("outer", "inner", "tensor"), None),
            P(("outer", "inner"), "tensor", None),
            P(("outer", "inner"), "tensor", None),
            P(("outer", "inner"), "tensor", None),
        ),
        check_vma=False,
    )
```
